128 devices in a mesh: pb: 2 (over y_lo), ka: 64 (over y_hi, x, z, core).
Axes of the slice: x: 4, y: 4 (y_hi: 2, y_lo: 2; y = y_hi * 2 + y_lo), z: 4, core: 2. Of those that a mesh axis runs over, the one named last changes fastest.
Arguments:
- queries: bfloat16 [512, 4096], P(('pb', 'ka')), may hold values from -44 to 44
- keys: bfloat16 [65536, 1024], P(('ka', 'pb')), may hold values from -6 to 6
- values: bfloat16 [65536, 1024], P(('ka', 'pb')), may hold values from -6 to 6
- grad_out: bfloat16 [512, 4096], P(('pb', 'ka')), may hold values from -6144 to 6144
- out: bfloat16 [512, 4096], P(('pb', 'ka')), may hold values from -6 to 6
- window_start: int32 [1], replicated, may hold values from 32768 to 65024
Outputs:
- grad_q: float32 [512, 4096], P(('pb', 'ka'))
- grad_k: float32 [65536, 1024], P(('ka', 'pb'))
- grad_v: float32 [65536, 1024], P(('ka', 'pb'))
The draws below stay inside these ranges and needn't reach their ends.
All inputs are finite; a program needn't handle non-finite values.
Results may differ from the reference program's by a relative error of at most 0.0029.
Values may be sent and summed in bfloat16 or wider, within the bound.
No kernel may reach another device: no remote copies, remote signals or barrier semaphores. Data moves between devices by JAX's collectives and lax.ppermute only.
A program may use at most 128 MiB of HBM per device.

```python
import math
import jax
import jax.numpy as jnp
from jax import lax

HEADS = 32
KV_HEADS = 8
HEAD_DIM = 128
KEY_DEV = 512
WINDOW = 512
CONTEXT = 65536
N_PB = 2


def draw_queries(key, part):
    key = jax.random.fold_in(key, 11)
    return jnp.clip(jax.random.normal(key, (WINDOW, HEADS * HEAD_DIM), jnp.float32), -6.0, 6.0).astype(jnp.bfloat16)


def draw_keys(key, part):
    key = jax.random.fold_in(key, 12)
    return jnp.clip(jax.random.normal(key, (CONTEXT, KV_HEADS * HEAD_DIM), jnp.float32), -6.0, 6.0).astype(jnp.bfloat16)


def shard_levels(key, extent, split, low, top_value):
    def one(dim, shards_of):
        steps = jax.random.uniform(jax.random.fold_in(jax.random.fold_in(key, 6), dim), (shards_of,), jnp.float32, low / len(split), top_value / len(split))
        return jnp.repeat(jnp.exp(steps), extent[dim] // shards_of).reshape((-1,) + (1,) * (len(extent) - dim - 1))

    level = one(*split[0])
    for cut in split[1:]:
        level = level * one(*cut)
    return level


def bell_draw(rng, dims, width, bound, split=(), kind=jnp.bfloat16):
    values = width * jax.random.normal(rng, dims, jnp.float32)
    if split:
        values = values * shard_levels(rng, dims, split, -0.22, 0.18)
    return jnp.clip(values, -bound, bound).astype(kind)


def setup_inputs(seed: int = 0) -> dict:
    seeds = jax.random.split(jax.random.key(seed), 7)
    return {
        "queries": draw_queries(jax.random.fold_in(seeds[6], 71), 0),
        "keys": draw_keys(jax.random.fold_in(seeds[6], 71), 0),
        "values": bell_draw(seeds[2], (CONTEXT, KV_HEADS * HEAD_DIM), 1.0, 6.0, ((0, 128),)),
        "grad_out": bell_draw(seeds[3], (WINDOW, HEADS * HEAD_DIM), (CONTEXT // 64), 6144.0, ((0, 128),)),
        "out": bell_draw(seeds[4], (WINDOW, HEADS * HEAD_DIM), 1.0, 6.0, ((0, 128),)),
        "window_start": jax.random.randint(seeds[5], (1,), CONTEXT // 2, CONTEXT - WINDOW + 1).astype(jnp.int32),
    }


MASKED = -1e+30

def reference(queries, keys, values, grad_out, out, window_start):
    inv_root = 1.0 / math.sqrt(HEAD_DIM)
    per_group = HEADS // KV_HEADS
    block = KEY_DEV * N_PB
    blocks = CONTEXT // block
    q_all = queries.reshape(WINDOW, KV_HEADS, per_group, HEAD_DIM).transpose(1, 0, 2, 3)
    do_all = grad_out.reshape(WINDOW, KV_HEADS, per_group, HEAD_DIM).transpose(1, 0, 2, 3)
    o_all = out.reshape(WINDOW, KV_HEADS, per_group, HEAD_DIM).transpose(1, 0, 2, 3)
    k_all = keys.reshape(blocks, block, KV_HEADS, HEAD_DIM).transpose(2, 0, 1, 3)
    v_all = values.reshape(blocks, block, KV_HEADS, HEAD_DIM).transpose(2, 0, 1, 3)
    query_pos = window_start[0] + jnp.arange(WINDOW, dtype=jnp.int32)
    block_ids = jnp.arange(blocks, dtype=jnp.int32)

    def one_group(inputs):
        q_group, do_group, o_group, k_group, v_group = inputs
        q_float = q_group.astype(jnp.float32)
        do_float = do_group.astype(jnp.float32)
        row_dots = lax.optimization_barrier(jnp.sum(do_float * o_group.astype(jnp.float32), axis=-1)).T

        def scores_of(key_block, block_index):
            key_pos = block_index * block + jnp.arange(block, dtype=jnp.int32)
            visible = key_pos[None, :] <= query_pos[:, None]
            scores = jnp.einsum('rhd,md->hrm', q_float, key_block.astype(jnp.float32)) * inv_root
            return (scores, visible)

        def stats_step(running, inputs_block):
            old_max, old_sum = running
            key_block, block_index = inputs_block
            scores, visible = scores_of(key_block, block_index)
            scores = jnp.where(visible[None], scores, MASKED)
            new_max = jnp.maximum(old_max, lax.optimization_barrier(jnp.max(scores, axis=-1)))
            fresh = lax.optimization_barrier(jnp.sum(jnp.where(visible[None], jnp.exp(scores - new_max[..., None]), 0.0), axis=-1))
            new_sum = old_sum * jnp.exp(old_max - new_max) + fresh
            return ((new_max, new_sum), None)
        start = (jnp.full((per_group, WINDOW), MASKED, jnp.float32), jnp.zeros((per_group, WINDOW), jnp.float32))
        (row_max, row_sum), _ = lax.scan(stats_step, start, (k_group, block_ids))
        log_totals = row_max + jnp.log(row_sum)

        def grad_step(query_acc, inputs_block):
            key_block, value_block, block_index = inputs_block
            scores, visible = scores_of(key_block, block_index)
            weights = jnp.where(visible[None], jnp.exp(scores - log_totals[..., None]), 0.0)
            weights_low = weights.astype(jnp.bfloat16)
            dweights = jnp.einsum('rhd,md->hrm', do_float, value_block.astype(jnp.float32))
            dscores = (weights * (dweights - row_dots[..., None])).astype(jnp.bfloat16).astype(jnp.float32)
            query_acc = query_acc + jnp.einsum('hrm,md->rhd', dscores, key_block.astype(jnp.float32)) * inv_root
            key_part = jnp.einsum('hrm,rhd->md', dscores, q_float) * inv_root
            value_part = jnp.einsum('hrm,rhd->md', weights_low.astype(jnp.float32), do_float)
            return (query_acc, (key_part, value_part))
        query_zero = jnp.zeros((WINDOW, per_group, HEAD_DIM), jnp.float32)
        query_acc, (key_parts, value_parts) = lax.scan(grad_step, query_zero, (k_group, v_group, block_ids))
        return (query_acc, key_parts, value_parts)
    query_acc, key_parts, value_parts = lax.map(one_group, (q_all, do_all, o_all, k_all, v_all))
    grad_q = query_acc.transpose(1, 0, 2, 3).reshape(WINDOW, HEADS * HEAD_DIM)
    grad_k = key_parts.transpose(1, 2, 0, 3).reshape(CONTEXT, KV_HEADS * HEAD_DIM)
    grad_v = value_parts.transpose(1, 2, 0, 3).reshape(CONTEXT, KV_HEADS * HEAD_DIM)
    return (grad_q, grad_k, grad_v)
```

```python
import functools
import math

import jax
import jax.numpy as jnp
from jax import lax
from jax.experimental import pallas as pl
from jax.experimental.pallas import tpu as pltpu
from jax.sharding import PartitionSpec as P

HEADS = 32
KV_HEADS = 8
HEAD_DIM = 128
PER_GROUP = HEADS // KV_HEADS
BOTH = ("pb", "ka")
DEVICES = 128
RINGS = 4
ROWS = 4
PAIRS = ROWS * PER_GROUP
MSG = 2 * PAIRS
PLANE = DEVICES // KV_HEADS
ALL_PAIRS = DEVICES * PAIRS
BLOCK = 512
EXTRA = 16
TALL = BLOCK + EXTRA
GRADS_COST = 0.1
JOIN_COST = 0.3
STATS_COST = 0.1
FIRST_COST = 12
PICK_KEYS_COST = 10
PICK_VALUES_COST = 0.1
STAT = 24
MASKED = -1e30
SAFE = 2.0**60
LOG2E = math.log2(math.e)
INV_ROOT = 1.0 / math.sqrt(HEAD_DIM)
SCALE2 = INV_ROOT * LOG2E
CHUNK = 512
F32 = jnp.float32
BF16 = jnp.bfloat16
VMEM = pltpu.CompilerParams(vmem_limit_bytes=20 * 1024 * 1024)
MOST_VMEM = pltpu.CompilerParams(vmem_limit_bytes=60 * 1024 * 1024)
HBM = pl.BlockSpec(memory_space=pl.ANY)
RING_GROUPS = [[s * KV_HEADS + g for g in range(KV_HEADS)] for s in range(PLANE)]
PLANE_GROUPS = [[s * KV_HEADS + g for s in range(PLANE)] for g in range(KV_HEADS)]


def cost(microseconds):
    return pl.CostEstimate(
        flops=int(microseconds * 5e8), bytes_accessed=int(microseconds * 2e6), transcendentals=0
    )


def any_block(*shape):
    return pl.BlockSpec(shape, lambda i, w: (0,) * len(shape))


def block_first(pos_ref, d, other):
    place = lax.rem(pos_ref[2] + RINGS - d, RINGS) * 2 + (pos_ref[3] ^ other)
    return pos_ref[1] + place * (2 * BLOCK)


def column_copies(where, src, outs, sems):
    copies = []
    for step in range(KV_HEADS):
        d, core = step // 2, step % 2
        first = (lax.rem(where[0] + d, RINGS) * 2 + core) * HEAD_DIM
        cols = pl.ds(pl.multiple_of(first, HEAD_DIM), HEAD_DIM)
        copies.append(
            pltpu.make_async_copy(
                src.at[:, cols], outs[d].at[core, pl.ds(0, BLOCK)], sems.at[step]
            )
        )
    return copies


def split_values_kernel(where, v_ref, *rest):
    copies = column_copies(where, v_ref, rest[:-1], rest[-1])
    for copy in copies:
        copy.start()
    for copy in copies:
        copy.wait()


def split_values(where, values):
    return pl.pallas_call(
        split_values_kernel,
        grid_spec=pltpu.PrefetchScalarGridSpec(
            num_scalar_prefetch=1,
            grid=(1,),
            in_specs=[any_block(BLOCK, KV_HEADS * HEAD_DIM)],
            out_specs=[HBM] * RINGS,
            scratch_shapes=[pltpu.SemaphoreType.DMA((KV_HEADS,))],
        ),
        out_shape=[jax.ShapeDtypeStruct((2, BLOCK, HEAD_DIM), BF16)] * RINGS,
        name="split_values",
        cost_estimate=cost(2),
    )(where, values)


def split_keys_kernel(where, k_ref, do_ref, o_ref, *rest):
    outs, (dots_ref, sems, dots_sems) = rest[:RINGS], rest[RINGS:]
    copies = column_copies(where, k_ref, outs, sems)
    for copy in copies:
        copy.start()
    products = do_ref[...].astype(F32) * o_ref[...].astype(F32)
    row = lax.broadcasted_iota(jnp.int32, (ROWS, HEAD_DIM), 0)
    me = where[0] * 2 + where[1]
    lane = lax.broadcasted_iota(jnp.int32, (ROWS, HEAD_DIM), 1) - me * PAIRS
    for g in range(KV_HEADS):
        line = jnp.zeros((1, HEAD_DIM), F32)
        for j in range(PER_GROUP):
            first = (g * PER_GROUP + j) * HEAD_DIM
            dots = jnp.sum(products[:, first : first + HEAD_DIM], axis=1, keepdims=True)
            placed = jnp.where(lane == row + j * ROWS, dots, 0.0)
            line += jnp.sum(placed, axis=0, keepdims=True)
        high = line.astype(BF16).astype(F32)
        rest_line = line - high
        middle = rest_line.astype(BF16).astype(F32)
        low = rest_line - middle
        rows = jnp.concatenate([high, middle, low, jnp.zeros((EXTRA - 3, HEAD_DIM), F32)], axis=0)
        dots_ref[g // 2, g % 2] = rows.astype(BF16)
    last = [
        pltpu.make_async_copy(
            dots_ref.at[lax.rem(where[0] + d, RINGS)],
            outs[d].at[:, pl.ds(BLOCK, EXTRA)],
            dots_sems.at[d],
        )
        for d in range(RINGS)
    ]
    for copy in last:
        copy.start()
    for copy in copies + last:
        copy.wait()


def split_keys(where, keys, grad_out, out):
    rows = any_block(ROWS, HEADS * HEAD_DIM)
    return pl.pallas_call(
        split_keys_kernel,
        grid_spec=pltpu.PrefetchScalarGridSpec(
            num_scalar_prefetch=1,
            grid=(1,),
            in_specs=[any_block(BLOCK, KV_HEADS * HEAD_DIM), rows, rows],
            out_specs=[HBM] * RINGS,
            scratch_shapes=[
                pltpu.VMEM((RINGS, 2, EXTRA, HEAD_DIM), BF16),
                pltpu.SemaphoreType.DMA((KV_HEADS,)),
                pltpu.SemaphoreType.DMA((RINGS,)),
            ],
        ),
        out_shape=[jax.ShapeDtypeStruct((2, TALL, HEAD_DIM), BF16)] * RINGS,
        name="split_keys",
        cost_estimate=cost(2),
    )(where, keys, grad_out, out)


def pick_kernel(where, *refs):
    for d in range(RINGS):
        refs[RINGS][d] = refs[d][0]


def pick_theirs(where, arrived, name, time):
    rest = arrived[0].shape[1:]
    return pl.pallas_call(
        pick_kernel,
        grid_spec=pltpu.PrefetchScalarGridSpec(
            num_scalar_prefetch=1,
            grid=(1,),
            in_specs=[pl.BlockSpec((1,) + rest, lambda i, w: (1 - w[1], 0, 0))] * RINGS,
            out_specs=any_block(RINGS, *rest),
        ),
        out_shape=jax.ShapeDtypeStruct((RINGS,) + rest, BF16),
        name=name,
        compiler_params=MOST_VMEM,
        cost_estimate=cost(time),
    )(where, *arrived)


def message_kernel(q_ref, do_ref, out_ref, part_ref, sems):
    q = q_ref[...].astype(F32)
    do = do_ref[...].astype(F32)
    for g in range(KV_HEADS):
        rows = []
        for source in (q, do):
            for j in range(PER_GROUP):
                first = (g * PER_GROUP + j) * HEAD_DIM
                rows.append(source[:, first : first + HEAD_DIM])
        part_ref[g] = jnp.concatenate(rows, axis=0).astype(BF16)
    copies = [
        pltpu.make_async_copy(part_ref, out_ref.at[s], sems.at[s]) for s in range(PLANE)
    ]
    for copy in copies:
        copy.start()
    for copy in copies:
        copy.wait()


def messages(queries, grad_out):
    return pl.pallas_call(
        message_kernel,
        out_specs=HBM,
        out_shape=jax.ShapeDtypeStruct((PLANE, KV_HEADS, MSG, HEAD_DIM), BF16),
        scratch_shapes=[
            pltpu.VMEM((KV_HEADS, MSG, HEAD_DIM), BF16),
            pltpu.SemaphoreType.DMA((PLANE,)),
        ],
        name="messages",
        cost_estimate=cost(2),
    )(queries, grad_out)


def pair_positions(first, count, start):
    index = first + lax.broadcasted_iota(jnp.int32, (1, count), 1)
    return start + (index // PAIRS) * ROWS + lax.rem(index, ROWS)


def nt_dot(a, b):
    return lax.dot_general(a, b, (((1,), (1,)), ((), ())), preferred_element_type=F32)


def nn_dot(a, b):
    return lax.dot_general(a, b, (((1,), (0,)), ((), ())), preferred_element_type=F32)


def tn_dot(a, b):
    return lax.dot_general(a, b, (((0,), (0,)), ((), ())), preferred_element_type=F32)


def stats_kernel(pos_ref, msg_ref, *refs):
    mine_refs, sib_ref = refs[:RINGS], refs[RINGS]
    out_ref, top_ref, sum_ref, fresh_ref, keys_ref, ready_ref = refs[RINGS + 1 :]
    start = pos_ref[0]
    top_ref[...] = jnp.full_like(top_ref, MASKED)
    sum_ref[...] = jnp.zeros_like(sum_ref)
    ready_ref[0] = 0
    terms = jnp.zeros((EXTRA, HEAD_DIM), F32)
    for d in range(RINGS):
        keys_ref[d] = mine_refs[d][0, 0:BLOCK]
        keys_ref[RINGS + d] = sib_ref[d, 0:BLOCK]
        terms += mine_refs[d][0, BLOCK:TALL].astype(F32) + sib_ref[d, BLOCK:TALL].astype(F32)

    def one(i, _):
        first = block_first(pos_ref, lax.rem(i, RINGS), i // RINGS)
        stats_step(
            first, start, msg_ref, lambda: keys_ref[i], top_ref, sum_ref, fresh_ref, ready_ref
        )

    lax.fori_loop(0, KV_HEADS, one, None)
    total = sum_ref[...]
    logs = jnp.where(total > 0.0, top_ref[...] + jnp.log2(jnp.maximum(total, 1e-37)), MASKED)
    rows = [logs[:, r * HEAD_DIM : (r + 1) * HEAD_DIM] for r in range(PAIRS)]
    rows.append(terms[0:1] + terms[1:2] + terms[2:3])
    rows.append(jnp.zeros((STAT - PAIRS - 1, HEAD_DIM), F32))
    out = jnp.concatenate(rows, axis=0)
    for s in range(PLANE):
        out_ref[s] = out


def stats_step(first, start, msg_ref, load, top_ref, sum_ref, fresh_ref, ready_ref):
    full = first + (BLOCK - 1) <= start
    some = first <= start + (DEVICES * ROWS - 1)

    def scores(c):
        devs = slice(c * CHUNK // PAIRS, (c + 1) * CHUNK // PAIRS)
        return nt_dot(load(), msg_ref[devs, 0:PAIRS].reshape(CHUNK, HEAD_DIM))

    def careful(masked):
        for c in range(ALL_PAIRS // CHUNK):
            cols = slice(c * CHUNK, (c + 1) * CHUNK)
            s = scores(c) * SCALE2
            if masked:
                key_pos = first + lax.broadcasted_iota(jnp.int32, (BLOCK, 1), 0)
                visible = key_pos <= pair_positions(c * CHUNK, CHUNK, start)
                s = jnp.where(visible, s, MASKED)
            old = top_ref[:, cols]
            top = jnp.maximum(old, jnp.max(s, axis=0, keepdims=True))
            e = jnp.exp2(s - top)
            if masked:
                e = jnp.where(visible, e, 0.0)
            sum_ref[:, cols] = sum_ref[:, cols] * jnp.exp2(old - top) + jnp.sum(
                e, axis=0, keepdims=True
            )
            top_ref[:, cols] = top

    quick = jnp.logical_and(full, ready_ref[0] == 1)

    @pl.when(quick)
    def _():
        for c in range(ALL_PAIRS // CHUNK):
            cols = slice(c * CHUNK, (c + 1) * CHUNK)
            e = jnp.exp2(scores(c) * SCALE2 - top_ref[:, cols])
            fresh_ref[:, cols] = jnp.sum(e, axis=0, keepdims=True)
        good = jnp.max(fresh_ref[...]) < SAFE

        @pl.when(good)
        def _():
            sum_ref[...] += fresh_ref[...]

        @pl.when(jnp.logical_not(good))
        def _():
            careful(False)

    @pl.when(jnp.logical_and(full, jnp.logical_not(quick)))
    def _():
        careful(False)
        ready_ref[0] = 1

    @pl.when(jnp.logical_and(some, jnp.logical_not(full)))
    def _():
        careful(True)


def stats(pos, msg, mine, sib):
    row = pltpu.VMEM((1, ALL_PAIRS), F32)
    return pl.pallas_call(
        stats_kernel,
        grid_spec=pltpu.PrefetchScalarGridSpec(
            num_scalar_prefetch=1,
            grid=(1,),
            in_specs=[any_block(DEVICES, MSG, HEAD_DIM)]
            + [pl.BlockSpec((1, TALL, HEAD_DIM), lambda i, p: (p[3], 0, 0))] * RINGS
            + [any_block(RINGS, TALL, HEAD_DIM)],
            out_specs=any_block(PLANE, STAT, HEAD_DIM),
            scratch_shapes=[
                row,
                row,
                row,
                pltpu.VMEM((KV_HEADS, BLOCK, HEAD_DIM), BF16),
                pltpu.SMEM((1,), jnp.int32),
            ],
        ),
        out_shape=jax.ShapeDtypeStruct((PLANE, STAT, HEAD_DIM), F32),
        name="stats",
        compiler_params=MOST_VMEM,
        cost_estimate=cost(STATS_COST),
    )(pos, msg, *mine, sib)


def grad_block(pos_ref, msg_ref, lines_ref, k_of, v_of, d, other, put, sum_ref):
    start = pos_ref[0]
    first = block_first(pos_ref, d, other)
    full = first + (BLOCK - 1) <= start
    some = first <= start + (DEVICES * ROWS - 1)

    def run(masked):
        k = k_of()
        v = v_of()
        dk = jnp.zeros((BLOCK, HEAD_DIM), F32)
        dv = jnp.zeros((BLOCK, HEAD_DIM), F32)
        for c in range(ALL_PAIRS // CHUNK):
            cols = slice(c * CHUNK, (c + 1) * CHUNK)
            devs = slice(c * CHUNK // PAIRS, (c + 1) * CHUNK // PAIRS)
            q = msg_ref[devs, 0:PAIRS].reshape(CHUNK, HEAD_DIM)
            do = msg_ref[devs, PAIRS:MSG].reshape(CHUNK, HEAD_DIM)
            w = jnp.exp2(nt_dot(k, q) * SCALE2 - lines_ref[0:1, cols])
            if masked:
                key_pos = first + lax.broadcasted_iota(jnp.int32, (BLOCK, 1), 0)
                visible = key_pos <= pair_positions(c * CHUNK, CHUNK, start)
                w = jnp.where(visible, w, 0.0)
            ds = (w * (nt_dot(v, do) - lines_ref[1:2, cols])).astype(BF16)
            dv += nn_dot(w.astype(BF16), do)
            dk += nn_dot(ds, q)
            sum_ref[cols, :] += tn_dot(ds, k)
        put((dk * INV_ROOT).astype(BF16), dv.astype(BF16))

    @pl.when(full)
    def _():
        run(False)

    @pl.when(jnp.logical_and(some, jnp.logical_not(full)))
    def _():
        run(True)

    @pl.when(jnp.logical_not(some))
    def _():
        zero = jnp.zeros((BLOCK, HEAD_DIM), BF16)
        put(zero, zero)


def first_kernel(pos_ref, msg_ref, stat_ref, k_ref, v_ref, g_ref, dq_ref, lines_ref):
    logs = stat_ref[:, 0:PAIRS]
    most = jnp.max(logs, axis=0)
    logs = most + jnp.log2(jnp.sum(jnp.exp2(logs - most), axis=0))
    for r in range(PLANE):
        cols = slice(r * HEAD_DIM, (r + 1) * HEAD_DIM)
        lines_ref[0:1, cols] = logs[r : r + 1]
        lines_ref[1:2, cols] = stat_ref[r, PAIRS : PAIRS + 1]
    dq_ref[...] = jnp.zeros_like(dq_ref)

    def put(dk, dv):
        g_ref[0, 0] = dk
        g_ref[0, 1] = dv

    grad_block(
        pos_ref, msg_ref, lines_ref, lambda: k_ref[0, 0:BLOCK], lambda: v_ref[0], 0, 0, put, dq_ref
    )


def first_grads(pos, msg, stat, k, v):
    return pl.pallas_call(
        first_kernel,
        grid_spec=pltpu.PrefetchScalarGridSpec(
            num_scalar_prefetch=1,
            grid=(1,),
            in_specs=[
                any_block(DEVICES, MSG, HEAD_DIM),
                any_block(PLANE, STAT, HEAD_DIM),
                pl.BlockSpec((1, TALL, HEAD_DIM), lambda i, p: (p[3], 0, 0)),
                pl.BlockSpec((1, BLOCK, HEAD_DIM), lambda i, p: (p[3], 0, 0)),
            ],
            out_specs=[
                any_block(1, 2, BLOCK, HEAD_DIM),
                any_block(ALL_PAIRS, HEAD_DIM),
                any_block(8, ALL_PAIRS),
            ],
        ),
        out_shape=[
            jax.ShapeDtypeStruct((1, 2, BLOCK, HEAD_DIM), BF16),
            jax.ShapeDtypeStruct((ALL_PAIRS, HEAD_DIM), F32),
            jax.ShapeDtypeStruct((8, ALL_PAIRS), F32),
        ],
        name="first_grads",
        compiler_params=VMEM,
        cost_estimate=cost(FIRST_COST),
    )(pos, msg, stat, k, v)


def sib_kernel(pos_ref, msg_ref, lines_ref, dq_in_ref, k_ref, v_ref, g_ref, dq_ref):
    dq_ref[...] = dq_in_ref[...]

    def one(d, _):
        def put(dk, dv):
            g_ref[d, 0] = dk
            g_ref[d, 1] = dv

        grad_block(
            pos_ref,
            msg_ref,
            lines_ref,
            lambda: k_ref[d, 0:BLOCK],
            lambda: v_ref[d],
            d,
            1,
            put,
            dq_ref,
        )

    lax.fori_loop(0, RINGS, one, None)


def sib_grads(pos, msg, lines, dq, k, v):
    return pl.pallas_call(
        sib_kernel,
        grid_spec=pltpu.PrefetchScalarGridSpec(
            num_scalar_prefetch=1,
            grid=(1,),
            in_specs=[
                any_block(DEVICES, MSG, HEAD_DIM),
                any_block(8, ALL_PAIRS),
                any_block(ALL_PAIRS, HEAD_DIM),
                any_block(RINGS, TALL, HEAD_DIM),
                any_block(RINGS, BLOCK, HEAD_DIM),
            ],
            out_specs=[any_block(RINGS, 2, BLOCK, HEAD_DIM), any_block(ALL_PAIRS, HEAD_DIM)],
        ),
        out_shape=[
            jax.ShapeDtypeStruct((RINGS, 2, BLOCK, HEAD_DIM), BF16),
            jax.ShapeDtypeStruct((ALL_PAIRS, HEAD_DIM), F32),
        ],
        name="sib_grads",
        compiler_params=VMEM,
        cost_estimate=cost(GRADS_COST),
    )(pos, msg, lines, dq, k, v)


def mine_kernel(d, pos_ref, msg_ref, lines_ref, dq_in_ref, k_ref, v_ref, other_ref, g_ref, dq_ref, sum_ref):
    slot = pos_ref[3]
    g_ref[1 - slot] = other_ref[0]
    sum_ref[...] = dq_in_ref[...]

    def put(dk, dv):
        g_ref[slot, 0] = dk
        g_ref[slot, 1] = dv

    grad_block(
        pos_ref, msg_ref, lines_ref, lambda: k_ref[0, 0:BLOCK], lambda: v_ref[0], d, 0, put, sum_ref
    )
    dq_ref[...] = sum_ref[...].astype(dq_ref.dtype)


def mine_grads(d, last, pos, msg, lines, dq, k, v, others):
    return pl.pallas_call(
        functools.partial(mine_kernel, d),
        grid_spec=pltpu.PrefetchScalarGridSpec(
            num_scalar_prefetch=1,
            grid=(1,),
            in_specs=[
                any_block(DEVICES, MSG, HEAD_DIM),
                any_block(8, ALL_PAIRS),
                any_block(ALL_PAIRS, HEAD_DIM),
                pl.BlockSpec((1, TALL, HEAD_DIM), lambda i, p: (p[3], 0, 0)),
                pl.BlockSpec((1, BLOCK, HEAD_DIM), lambda i, p: (p[3], 0, 0)),
                pl.BlockSpec((1, 2, BLOCK, HEAD_DIM), lambda i, p: (d, 0, 0, 0)),
            ],
            out_specs=[any_block(2, 2, BLOCK, HEAD_DIM), any_block(ALL_PAIRS, HEAD_DIM)],
            scratch_shapes=[pltpu.VMEM((ALL_PAIRS, HEAD_DIM), F32)],
        ),
        out_shape=[
            jax.ShapeDtypeStruct((2, 2, BLOCK, HEAD_DIM), BF16),
            jax.ShapeDtypeStruct((ALL_PAIRS, HEAD_DIM), BF16 if last else F32),
        ],
        name=f"mine_grads_{d}",
        compiler_params=VMEM,
        cost_estimate=cost(GRADS_COST),
    )(pos, msg, lines, dq, k, v, others)


def join_kernel(d, where, a_ref, b_ref, *refs):
    dk_ref, dv_ref, pair_ref, sems = refs[-4:]
    halves = [(where[1], a_ref.at[0]), (1 - where[1], b_ref.at[0])]
    if d:
        halves = [(0, a_ref.at[0]), (1, b_ref.at[0])]
    for core, block in halves:
        cols = pl.ds(pl.multiple_of(core * HEAD_DIM, HEAD_DIM), HEAD_DIM)
        pair_ref[0, :, cols] = block[0].astype(F32)
        pair_ref[1, :, cols] = block[1].astype(F32)
    first = lax.rem(where[0] + d, RINGS) * (2 * HEAD_DIM)
    cols = pl.ds(pl.multiple_of(first, 2 * HEAD_DIM), 2 * HEAD_DIM)
    copies = [
        pltpu.make_async_copy(pair_ref.at[i], ref.at[:, cols], sems.at[i])
        for i, ref in enumerate((dk_ref, dv_ref))
    ]
    for copy in copies:
        copy.start()
    for copy in copies:
        copy.wait()


def join_heads(d, where, part, others, outs):
    shape = jax.ShapeDtypeStruct((BLOCK, KV_HEADS * HEAD_DIM), F32)
    spec = pl.BlockSpec((1, 2, BLOCK, HEAD_DIM), lambda i, w: (0, 0, 0, 0))
    other_spec = pl.BlockSpec((1, 2, BLOCK, HEAD_DIM), lambda i, w: (1 if d else 0, 0, 0, 0))
    return pl.pallas_call(
        functools.partial(join_kernel, d),
        grid_spec=pltpu.PrefetchScalarGridSpec(
            num_scalar_prefetch=1,
            grid=(1,),
            in_specs=[spec, other_spec] + [HBM] * len(outs),
            out_specs=[HBM, HBM],
            scratch_shapes=[
                pltpu.VMEM((2, BLOCK, 2 * HEAD_DIM), F32),
                pltpu.SemaphoreType.DMA((2,)),
            ],
        ),
        out_shape=[shape, shape],
        input_output_aliases={3: 0, 4: 1} if outs else {},
        name=f"join_heads_{d}",
        compiler_params=VMEM,
        cost_estimate=cost(JOIN_COST),
    )(where, part, part if d else others, *outs)


def query_kernel(part_ref, out_ref):
    for g in range(KV_HEADS):
        total = part_ref[g].astype(F32)
        for s in range(1, DEVICES // KV_HEADS):
            total += part_ref[s * KV_HEADS + g].astype(F32)
        total = total * INV_ROOT
        for j in range(PER_GROUP):
            first = (g * PER_GROUP + j) * HEAD_DIM
            out_ref[:, first : first + HEAD_DIM] = total[j * ROWS : (j + 1) * ROWS]


def query_sum(parts):
    return pl.pallas_call(
        query_kernel,
        out_shape=jax.ShapeDtypeStruct((ROWS, HEADS * HEAD_DIM), F32),
        name="query_sum",
        compiler_params=VMEM,
    )(parts)


def swap(array, groups):
    return lax.all_to_all(array, BOTH, 0, 0, axis_index_groups=groups, tiled=True)


def z_route(turn):
    pairs = []
    for device in range(DEVICES):
        chip = (device // 2) % RINGS
        target = (chip + turn) % RINGS
        pairs.append((device, device + 2 * (target - chip)))
    return pairs


CORE_SWAP = [(device, device ^ 1) for device in range(DEVICES)]


def around(parts):
    return [parts[0]] + [lax.ppermute(parts[d], BOTH, z_route(d)) for d in range(1, RINGS)]


def local(queries, keys, values, grad_out, out, window_start):
    ka = lax.axis_index("ka")
    ring = lax.rem(ka, KV_HEADS)
    chip, core = ring // 2, lax.rem(ring, 2)
    first = ((ka - ring) * 2 + lax.axis_index("pb")) * BLOCK
    pos = jnp.stack([window_start[0], first, chip, core]).astype(jnp.int32)
    where = jnp.stack([chip, core]).astype(jnp.int32)

    k_parts = split_keys(where, keys, grad_out, out)
    k = around(k_parts)
    msg_out = messages(queries, grad_out)
    msg = swap(msg_out.reshape(DEVICES, MSG, HEAD_DIM), None)
    values, _ = lax.optimization_barrier((values, msg_out))
    v_parts = split_values(where, values)
    k, _ = lax.optimization_barrier((k, v_parts))
    v = around(v_parts)
    picked = pick_theirs(where, k, "pick_keys", PICK_KEYS_COST)
    k_sib = lax.ppermute(picked, BOTH, CORE_SWAP)
    msg, _ = lax.optimization_barrier((msg, picked))
    own_stat = stats(pos, msg, k, k_sib)
    stat = swap(own_stat, PLANE_GROUPS)
    v_picked = pick_theirs(where, v, "pick_values", PICK_VALUES_COST)
    v_sib = lax.ppermute(v_picked, BOTH, CORE_SWAP)

    part, dq, lines = first_grads(pos, msg, stat, k[0], v[0])
    back = [part] + [None] * (RINGS - 1)
    sib_parts, dq = sib_grads(pos, msg, lines, dq, k_sib, v_sib)
    others = lax.ppermute(sib_parts, BOTH, CORE_SWAP)
    order = (2, 1, 3)
    for d in order:
        part, dq = mine_grads(d, d == order[-1], pos, msg, lines, dq, k[d], v[d], others)
        back[d] = lax.ppermute(part, BOTH, z_route(-d))
    dq = swap(dq.reshape(DEVICES, PAIRS, HEAD_DIM), None)
    outs = ()
    for d in (0, 2, 1, 3):
        outs = join_heads(d, where, back[d], others, outs)
    dq, outs = lax.optimization_barrier((dq, outs))
    return query_sum(dq), outs[0], outs[1]


def solution(mesh):
    return jax.shard_map(
        local,
        mesh=mesh,
        in_specs=(
            P(("pb", "ka"), None),
            P(("ka", "pb"), None),
            P(("ka", "pb"), None),
            P(("pb", "ka"), None),
            P(("pb", "ka"), None),
            P(),
        ),
        out_specs=(P(("pb", "ka"), None), P(("ka", "pb"), None), P(("ka", "pb"), None)),
        check_vma=False,
    )
```

```python
import functools
import math

import jax
import jax.numpy as jnp
from jax import lax
from jax.experimental import pallas as pl
from jax.experimental.pallas import tpu as pltpu
from jax.sharding import PartitionSpec as P

HEADS = 32
KV_HEADS = 8
HEAD_DIM = 128
PER_GROUP = HEADS // KV_HEADS
BOTH = ("pb", "ka")
DEVICES = 128
RINGS = 4
ROWS = 4
PAIRS = ROWS * PER_GROUP
MSG = 2 * PAIRS
PLANE = DEVICES // KV_HEADS
ALL_PAIRS = DEVICES * PAIRS
BLOCK = 512
EXTRA = 16
TALL = BLOCK + EXTRA
GRADS_COST = 0.1
JOIN_COST = 0.3
STATS_COST = 0.1
FIRST_COST = 12
PICK_KEYS_COST = 10
PICK_VALUES_COST = 0.1
STAT = 24
MASKED = -1e30
SAFE = 2.0**60
LOG2E = math.log2(math.e)
INV_ROOT = 1.0 / math.sqrt(HEAD_DIM)
SCALE2 = INV_ROOT * LOG2E
CHUNK = 512
F32 = jnp.float32
BF16 = jnp.bfloat16
VMEM = pltpu.CompilerParams(vmem_limit_bytes=20 * 1024 * 1024)
LITTLE_VMEM = pltpu.CompilerParams(vmem_limit_bytes=10 * 1024 * 1024)
HBM = pl.BlockSpec(memory_space=pl.ANY)
RING_GROUPS = [[s * KV_HEADS + g for g in range(KV_HEADS)] for s in range(PLANE)]
PLANE_GROUPS = [[s * KV_HEADS + g for s in range(PLANE)] for g in range(KV_HEADS)]


def cost(microseconds):
    return pl.CostEstimate(
        flops=int(microseconds * 5e8), bytes_accessed=int(microseconds * 2e6), transcendentals=0
    )


SCALARS = pl.BlockSpec(memory_space=pltpu.SMEM)
WHOLE = pl.BlockSpec(memory_space=pltpu.VMEM)


def any_block(*shape):
    return pl.BlockSpec(shape, lambda i, w: (0,) * len(shape))


def block_first(pos_ref, d, other):
    place = lax.rem(pos_ref[0] + RINGS - d, RINGS) * 2 + (pos_ref[1] ^ other)
    return pos_ref[2] + place * (2 * BLOCK)


def column_copies(where, src, outs, sems):
    copies = []
    for step in range(KV_HEADS):
        d, core = step // 2, step % 2
        first = (lax.rem(where[0] + d, RINGS) * 2 + core) * HEAD_DIM
        cols = pl.ds(pl.multiple_of(first, HEAD_DIM), HEAD_DIM)
        copies.append(
            pltpu.make_async_copy(
                src.at[:, cols], outs[d].at[core, pl.ds(0, BLOCK)], sems.at[step]
            )
        )
    return copies


def split_values_kernel(where, v_ref, *rest):
    copies = column_copies(where, v_ref, rest[:-1], rest[-1])
    for copy in copies:
        copy.start()
    for copy in copies:
        copy.wait()


def split_values(where, values):
    return pl.pallas_call(
        split_values_kernel,
        grid_spec=pltpu.PrefetchScalarGridSpec(
            num_scalar_prefetch=1,
            grid=(1,),
            in_specs=[any_block(BLOCK, KV_HEADS * HEAD_DIM)],
            out_specs=[HBM] * RINGS,
            scratch_shapes=[pltpu.SemaphoreType.DMA((KV_HEADS,))],
        ),
        out_shape=[jax.ShapeDtypeStruct((2, BLOCK, HEAD_DIM), BF16)] * RINGS,
        name="split_values",
        cost_estimate=cost(2),
    )(where, values)


def split_keys_kernel(where, k_ref, do_ref, o_ref, *rest):
    outs, (dots_ref, sems, dots_sems) = rest[:RINGS], rest[RINGS:]
    copies = column_copies(where, k_ref, outs, sems)
    for copy in copies:
        copy.start()
    products = do_ref[...].astype(F32) * o_ref[...].astype(F32)
    row = lax.broadcasted_iota(jnp.int32, (ROWS, HEAD_DIM), 0)
    me = where[0] * 2 + where[1]
    lane = lax.broadcasted_iota(jnp.int32, (ROWS, HEAD_DIM), 1) - me * PAIRS
    for g in range(KV_HEADS):
        line = jnp.zeros((1, HEAD_DIM), F32)
        for j in range(PER_GROUP):
            first = (g * PER_GROUP + j) * HEAD_DIM
            dots = jnp.sum(products[:, first : first + HEAD_DIM], axis=1, keepdims=True)
            placed = jnp.where(lane == row + j * ROWS, dots, 0.0)
            line += jnp.sum(placed, axis=0, keepdims=True)
        high = line.astype(BF16).astype(F32)
        rest_line = line - high
        middle = rest_line.astype(BF16).astype(F32)
        low = rest_line - middle
        rows = jnp.concatenate([high, middle, low, jnp.zeros((EXTRA - 3, HEAD_DIM), F32)], axis=0)
        dots_ref[g // 2, g % 2] = rows.astype(BF16)
    last = [
        pltpu.make_async_copy(
            dots_ref.at[lax.rem(where[0] + d, RINGS)],
            outs[d].at[:, pl.ds(BLOCK, EXTRA)],
            dots_sems.at[d],
        )
        for d in range(RINGS)
    ]
    for copy in last:
        copy.start()
    for copy in copies + last:
        copy.wait()


def split_keys(where, keys, grad_out, out):
    rows = any_block(ROWS, HEADS * HEAD_DIM)
    return pl.pallas_call(
        split_keys_kernel,
        grid_spec=pltpu.PrefetchScalarGridSpec(
            num_scalar_prefetch=1,
            grid=(1,),
            in_specs=[any_block(BLOCK, KV_HEADS * HEAD_DIM), rows, rows],
            out_specs=[HBM] * RINGS,
            scratch_shapes=[
                pltpu.VMEM((RINGS, 2, EXTRA, HEAD_DIM), BF16),
                pltpu.SemaphoreType.DMA((KV_HEADS,)),
                pltpu.SemaphoreType.DMA((RINGS,)),
            ],
        ),
        out_shape=[jax.ShapeDtypeStruct((2, TALL, HEAD_DIM), BF16)] * RINGS,
        name="split_keys",
        cost_estimate=cost(2),
    )(where, keys, grad_out, out)


def pick_kernel(where, *refs):
    for d, ref in enumerate(refs[:-1]):
        refs[-1][d] = ref[0]


def pick_theirs(where, arrived, name, time):
    rest = arrived[0].shape[1:]
    zeros = (0,) * len(rest)
    return pl.pallas_call(
        pick_kernel,
        grid_spec=pltpu.PrefetchScalarGridSpec(
            num_scalar_prefetch=1,
            grid=(1,),
            in_specs=[pl.BlockSpec((1,) + rest, lambda i, w: (1 - w[1],) + zeros)] * len(arrived),
            out_specs=any_block(len(arrived), *rest),
        ),
        out_shape=jax.ShapeDtypeStruct((len(arrived),) + rest, BF16),
        name=name,
        compiler_params=LITTLE_VMEM,
        cost_estimate=cost(time),
    )(where, *arrived)


def message_kernel(q_ref, do_ref, out_ref, part_ref, sems):
    q = q_ref[...].astype(F32)
    do = do_ref[...].astype(F32)
    for g in range(KV_HEADS):
        rows = []
        for source in (q, do):
            for j in range(PER_GROUP):
                first = (g * PER_GROUP + j) * HEAD_DIM
                rows.append(source[:, first : first + HEAD_DIM])
        part_ref[g] = jnp.concatenate(rows, axis=0).astype(BF16)
    copies = [
        pltpu.make_async_copy(part_ref, out_ref.at[s], sems.at[s]) for s in range(PLANE)
    ]
    for copy in copies:
        copy.start()
    for copy in copies:
        copy.wait()


def messages(queries, grad_out):
    return pl.pallas_call(
        message_kernel,
        out_specs=HBM,
        out_shape=jax.ShapeDtypeStruct((PLANE, KV_HEADS, MSG, HEAD_DIM), BF16),
        scratch_shapes=[
            pltpu.VMEM((KV_HEADS, MSG, HEAD_DIM), BF16),
            pltpu.SemaphoreType.DMA((PLANE,)),
        ],
        name="messages",
        cost_estimate=cost(2),
    )(queries, grad_out)


def pair_positions(first, count, start):
    index = first + lax.broadcasted_iota(jnp.int32, (1, count), 1)
    return start + (index // PAIRS) * ROWS + lax.rem(index, ROWS)


def nt_dot(a, b):
    return lax.dot_general(a, b, (((1,), (1,)), ((), ())), preferred_element_type=F32)


def nn_dot(a, b):
    return lax.dot_general(a, b, (((1,), (0,)), ((), ())), preferred_element_type=F32)


def stats_kernel(pos_ref, msg_ref, *refs):
    mine_refs, sib_ref = refs[:RINGS], refs[RINGS]
    core = pos_ref[1]
    out_ref, top_ref, sum_ref, fresh_ref, keys_ref, ready_ref = refs[RINGS + 1 :]
    start = pos_ref[3]
    top_ref[...] = jnp.full_like(top_ref, MASKED)
    sum_ref[...] = jnp.zeros_like(sum_ref)
    ready_ref[0] = 0
    terms = jnp.zeros((EXTRA, HEAD_DIM), F32)
    for d in range(RINGS):
        keys_ref[d] = mine_refs[d][core, 0:BLOCK]
        keys_ref[RINGS + d] = sib_ref[d, 0:BLOCK]
        terms += mine_refs[d][core, BLOCK:TALL].astype(F32) + sib_ref[d, BLOCK:TALL].astype(F32)

    def one(i, _):
        first = block_first(pos_ref, lax.rem(i, RINGS), i // RINGS)
        stats_step(
            first, start, msg_ref, lambda: keys_ref[i], top_ref, sum_ref, fresh_ref, ready_ref
        )

    lax.fori_loop(0, KV_HEADS, one, None)
    total = sum_ref[...]
    logs = jnp.where(total > 0.0, top_ref[...] + jnp.log2(jnp.maximum(total, 1e-37)), MASKED)
    rows = [logs[:, r * HEAD_DIM : (r + 1) * HEAD_DIM] for r in range(PAIRS)]
    rows.append(terms[0:1] + terms[1:2] + terms[2:3])
    rows.append(jnp.zeros((STAT - PAIRS - 1, HEAD_DIM), F32))
    out = jnp.concatenate(rows, axis=0)
    for s in range(PLANE):
        out_ref[s] = out


def stats_step(first, start, msg_ref, load, top_ref, sum_ref, fresh_ref, ready_ref):
    full = first + (BLOCK - 1) <= start
    some = first <= start + (DEVICES * ROWS - 1)

    def scores(c):
        devs = slice(c * CHUNK // PAIRS, (c + 1) * CHUNK // PAIRS)
        return nt_dot(load(), msg_ref[devs, 0:PAIRS].reshape(CHUNK, HEAD_DIM))

    def careful(masked):
        for c in range(ALL_PAIRS // CHUNK):
            cols = slice(c * CHUNK, (c + 1) * CHUNK)
            s = scores(c) * SCALE2
            if masked:
                key_pos = first + lax.broadcasted_iota(jnp.int32, (BLOCK, 1), 0)
                visible = key_pos <= pair_positions(c * CHUNK, CHUNK, start)
                s = jnp.where(visible, s, MASKED)
            old = top_ref[:, cols]
            top = jnp.maximum(old, jnp.max(s, axis=0, keepdims=True))
            e = jnp.exp2(s - top)
            if masked:
                e = jnp.where(visible, e, 0.0)
            sum_ref[:, cols] = sum_ref[:, cols] * jnp.exp2(old - top) + jnp.sum(
                e, axis=0, keepdims=True
            )
            top_ref[:, cols] = top

    quick = jnp.logical_and(full, ready_ref[0] == 1)

    @pl.when(quick)
    def _():
        for c in range(ALL_PAIRS // CHUNK):
            cols = slice(c * CHUNK, (c + 1) * CHUNK)
            e = jnp.exp2(scores(c) * SCALE2 - top_ref[:, cols])
            fresh_ref[:, cols] = jnp.sum(e, axis=0, keepdims=True)
        good = jnp.max(fresh_ref[...]) < SAFE

        @pl.when(good)
        def _():
            sum_ref[...] += fresh_ref[...]

        @pl.when(jnp.logical_not(good))
        def _():
            careful(False)

    @pl.when(jnp.logical_and(full, jnp.logical_not(quick)))
    def _():
        careful(False)
        ready_ref[0] = 1

    @pl.when(jnp.logical_and(some, jnp.logical_not(full)))
    def _():
        careful(True)


def stats(pos, msg, mine, sib):
    row = pltpu.VMEM((1, ALL_PAIRS), F32)
    return pl.pallas_call(
        stats_kernel,
        in_specs=[SCALARS] + [WHOLE] * (2 + RINGS),
        out_specs=WHOLE,
        scratch_shapes=[
            row,
            row,
            row,
            pltpu.VMEM((KV_HEADS, BLOCK, HEAD_DIM), BF16),
            pltpu.SMEM((1,), jnp.int32),
        ],
        out_shape=jax.ShapeDtypeStruct((PLANE, STAT, HEAD_DIM), F32),
        name="stats",
        compiler_params=VMEM,
        cost_estimate=cost(STATS_COST),
    )(pos, msg, *mine, sib)


def grad_block(pos_ref, msg_ref, lines_ref, k_of, v_of, d, other, put, sum_ref):
    start = pos_ref[3]
    first = block_first(pos_ref, d, other)
    full = first + (BLOCK - 1) <= start
    some = first <= start + (DEVICES * ROWS - 1)

    def run(masked):
        k = k_of()
        v = v_of()
        k_turned = k.astype(F32).T.astype(BF16)
        dk = jnp.zeros((BLOCK, HEAD_DIM), F32)
        dv = jnp.zeros((BLOCK, HEAD_DIM), F32)
        for c in range(ALL_PAIRS // CHUNK):
            cols = slice(c * CHUNK, (c + 1) * CHUNK)
            devs = slice(c * CHUNK // PAIRS, (c + 1) * CHUNK // PAIRS)
            q = msg_ref[devs, 0:PAIRS].reshape(CHUNK, HEAD_DIM)
            do = msg_ref[devs, PAIRS:MSG].reshape(CHUNK, HEAD_DIM)
            w = jnp.exp2(nt_dot(k, q) * SCALE2 - lines_ref[0:1, cols])
            if masked:
                key_pos = first + lax.broadcasted_iota(jnp.int32, (BLOCK, 1), 0)
                visible = key_pos <= pair_positions(c * CHUNK, CHUNK, start)
                w = jnp.where(visible, w, 0.0)
            ds = (w * (nt_dot(v, do) - lines_ref[1:2, cols])).astype(BF16)
            dv += nn_dot(w.astype(BF16), do)
            dk += nn_dot(ds, q)
            sum_ref[:, cols] += nn_dot(k_turned, ds)
        put((dk * INV_ROOT).astype(BF16), dv.astype(BF16))

    @pl.when(full)
    def _():
        run(False)

    @pl.when(jnp.logical_and(some, jnp.logical_not(full)))
    def _():
        run(True)

    @pl.when(jnp.logical_not(some))
    def _():
        zero = jnp.zeros((BLOCK, HEAD_DIM), BF16)
        put(zero, zero)


PAIR_SHAPE = jax.ShapeDtypeStruct((2, 2, BLOCK, HEAD_DIM), BF16)
DQ_SHAPE = jax.ShapeDtypeStruct((HEAD_DIM, ALL_PAIRS), F32)


def first_kernel(d, pos_ref, msg_ref, stat_ref, k_ref, v_ref, g_ref, dq_ref, lines_ref):
    core = pos_ref[1]
    logs = stat_ref[:, 0:PAIRS]
    most = jnp.max(logs, axis=0)
    logs = most + jnp.log2(jnp.sum(jnp.exp2(logs - most), axis=0))
    for r in range(PLANE):
        cols = slice(r * HEAD_DIM, (r + 1) * HEAD_DIM)
        lines_ref[0:1, cols] = logs[r : r + 1]
        lines_ref[1:2, cols] = stat_ref[r, PAIRS : PAIRS + 1]
    dq_ref[...] = jnp.zeros_like(dq_ref)

    def put(dk, dv):
        g_ref[0, 0] = dk
        g_ref[0, 1] = dv

    grad_block(
        pos_ref, msg_ref, lines_ref, lambda: k_ref[core, 0:BLOCK], lambda: v_ref[core], d, 0, put, dq_ref
    )


def first_grads(d, pos, msg, stat, k, v):
    return pl.pallas_call(
        functools.partial(first_kernel, d),
        in_specs=[SCALARS] + [WHOLE] * 4,
        out_specs=[WHOLE] * 3,
        out_shape=[
            jax.ShapeDtypeStruct((1, 2, BLOCK, HEAD_DIM), BF16),
            DQ_SHAPE,
            jax.ShapeDtypeStruct((8, ALL_PAIRS), F32),
        ],
        name="first_grads",
        compiler_params=VMEM,
        cost_estimate=cost(FIRST_COST),
    )(pos, msg, stat, k, v)


def pair_kernel(d, early, pos_ref, msg_ref, lines_ref, dq_in_ref, *refs):
    refs = list(refs)
    core = pos_ref[1]
    dq_ref, g_ref = refs[-1], refs[-2]
    dq_ref[...] = dq_in_ref[...]

    def block(k_of, v_of, other):
        slot = 1 - core if other else core

        def put(dk, dv):
            g_ref[slot, 0] = dk
            g_ref[slot, 1] = dv

        grad_block(pos_ref, msg_ref, lines_ref, k_of, v_of, d, other, put, dq_ref)

    ks_ref, vs_ref = refs[0], refs[1]
    block(lambda: ks_ref[d, 0:BLOCK], lambda: vs_ref[d], 1)
    if early:
        g_ref[core] = refs[2][0]
    else:
        k_ref, v_ref = refs[2], refs[3]
        block(lambda: k_ref[core, 0:BLOCK], lambda: v_ref[core], 0)


def pair_grads(d, pos, msg, lines, dq, k_sib, v_sib, own):
    return pl.pallas_call(
        functools.partial(pair_kernel, d, len(own) == 1),
        in_specs=[SCALARS] + [WHOLE] * (5 + len(own)),
        out_specs=[WHOLE] * 2,
        out_shape=[PAIR_SHAPE, DQ_SHAPE],
        input_output_aliases={3: 1},
        name=f"pair_grads_{d}",
        compiler_params=VMEM,
        cost_estimate=cost(GRADS_COST),
    )(pos, msg, lines, dq, k_sib, v_sib, *own)


def last_kernel(pos_ref, msg_ref, lines_ref, dq_in_ref, ks_ref, vs_ref, k_ref, v_ref, came_ref, *refs):
    own_ref, their_ref, dq_ref, sum_ref = refs
    core = pos_ref[1]
    sum_ref[...] = dq_in_ref[...]
    their_ref[1] = came_ref[1 - core]

    def put_theirs(dk, dv):
        their_ref[0, 0] = dk
        their_ref[0, 1] = dv

    def put_own(dk, dv):
        own_ref[0, 0] = dk
        own_ref[0, 1] = dv

    grad_block(
        pos_ref, msg_ref, lines_ref, lambda: ks_ref[0, 0:BLOCK], lambda: vs_ref[0], 0, 1, put_theirs, sum_ref
    )
    grad_block(
        pos_ref, msg_ref, lines_ref, lambda: k_ref[core, 0:BLOCK], lambda: v_ref[core], 0, 0, put_own, sum_ref
    )
    dq_ref[...] = sum_ref[...].T.astype(dq_ref.dtype)


def last_grads(pos, msg, lines, dq, k_sib, v_sib, k, v, came):
    return pl.pallas_call(
        last_kernel,
        in_specs=[SCALARS] + [WHOLE] * 8,
        out_specs=[WHOLE] * 3,
        scratch_shapes=[pltpu.VMEM((HEAD_DIM, ALL_PAIRS), F32)],
        out_shape=[
            jax.ShapeDtypeStruct((1, 2, BLOCK, HEAD_DIM), BF16),
            PAIR_SHAPE,
            jax.ShapeDtypeStruct((ALL_PAIRS, HEAD_DIM), BF16),
        ],
        name="last_grads",
        compiler_params=VMEM,
        cost_estimate=cost(GRADS_COST),
    )(pos, msg, lines, dq, k_sib, v_sib, k, v, came)


def join_kernel(chips, where, *refs):
    dk_ref, dv_ref, pair_ref, sems = refs[-4:]
    copies = []
    for n, d in enumerate(chips):
        for core, ref in ((where[1], refs[2 * n]), (1 - where[1], refs[2 * n + 1])):
            cols = pl.ds(pl.multiple_of(core * HEAD_DIM, HEAD_DIM), HEAD_DIM)
            pair_ref[n, 0, :, cols] = ref[0, 0].astype(F32)
            pair_ref[n, 1, :, cols] = ref[0, 1].astype(F32)
        first = lax.rem(where[0] + d, RINGS) * (2 * HEAD_DIM)
        cols = pl.ds(pl.multiple_of(first, 2 * HEAD_DIM), 2 * HEAD_DIM)
        for i, ref in enumerate((dk_ref, dv_ref)):
            copies.append(
                pltpu.make_async_copy(pair_ref.at[n, i], ref.at[:, cols], sems.at[n, i])
            )
            copies[-1].start()
    for copy in copies:
        copy.wait()


def join_heads(chips, where, parts, theirs, outs):
    shape = jax.ShapeDtypeStruct((BLOCK, KV_HEADS * HEAD_DIM), F32)
    operands, specs = [], []
    for part, (array, at) in zip(parts, theirs):
        operands += [part, array]
        if part.shape[0] == 2:
            specs.append(pl.BlockSpec((1, 2, BLOCK, HEAD_DIM), lambda i, w: (w[1], 0, 0, 0)))
        else:
            specs.append(any_block(1, 2, BLOCK, HEAD_DIM))
        specs.append(pl.BlockSpec((1, 2, BLOCK, HEAD_DIM), lambda i, w, at=at: (at, 0, 0, 0)))
    count = len(operands)
    return pl.pallas_call(
        functools.partial(join_kernel, chips),
        grid_spec=pltpu.PrefetchScalarGridSpec(
            num_scalar_prefetch=1,
            grid=(1,),
            in_specs=specs + [HBM] * len(outs),
            out_specs=[HBM, HBM],
            scratch_shapes=[
                pltpu.VMEM((2, 2, BLOCK, 2 * HEAD_DIM), F32),
                pltpu.SemaphoreType.DMA((2, 2)),
            ],
        ),
        out_shape=[shape, shape],
        input_output_aliases={1 + count: 0, 2 + count: 1} if outs else {},
        name=f"join_heads_{chips[0]}",
        compiler_params=VMEM,
        cost_estimate=cost(JOIN_COST),
    )(where, *operands, *outs)


def query_kernel(part_ref, out_ref):
    for g in range(KV_HEADS):
        total = part_ref[g].astype(F32)
        for s in range(1, DEVICES // KV_HEADS):
            total += part_ref[s * KV_HEADS + g].astype(F32)
        total = total * INV_ROOT
        for j in range(PER_GROUP):
            first = (g * PER_GROUP + j) * HEAD_DIM
            out_ref[:, first : first + HEAD_DIM] = total[j * ROWS : (j + 1) * ROWS]


def query_sum(parts):
    return pl.pallas_call(
        query_kernel,
        out_shape=jax.ShapeDtypeStruct((ROWS, HEADS * HEAD_DIM), F32),
        name="query_sum",
        compiler_params=VMEM,
    )(parts)


def swap(array, groups):
    return lax.all_to_all(array, BOTH, 0, 0, axis_index_groups=groups, tiled=True)


def z_route(turn):
    pairs = []
    for device in range(DEVICES):
        chip = (device // 2) % RINGS
        target = (chip + turn) % RINGS
        pairs.append((device, device + 2 * (target - chip)))
    return pairs


CORE_SWAP = [(device, device ^ 1) for device in range(DEVICES)]


def around(parts):
    return [parts[0]] + [lax.ppermute(parts[d], BOTH, z_route(d)) for d in range(1, RINGS)]


def local(queries, keys, values, grad_out, out, window_start):
    ka = lax.axis_index("ka")
    ring = lax.rem(ka, KV_HEADS)
    chip, core = ring // 2, lax.rem(ring, 2)
    first = ((ka - ring) * 2 + lax.axis_index("pb")) * BLOCK
    where = jnp.stack([chip, core, first, window_start[0]]).astype(jnp.int32)

    k_parts = split_keys(where, keys, grad_out, out)
    k = around(k_parts)
    msg_out = messages(queries, grad_out)
    msg = swap(msg_out.reshape(DEVICES, MSG, HEAD_DIM), None)
    values, _ = lax.optimization_barrier((values, msg_out))
    v_parts = split_values(where, values)
    k, _ = lax.optimization_barrier((k, v_parts))
    v = around(v_parts)
    picked = pick_theirs(where, k, "pick_keys", PICK_KEYS_COST)
    k_sib = lax.ppermute(picked, BOTH, CORE_SWAP)
    msg, _ = lax.optimization_barrier((msg, picked))
    own_stat = stats(where, msg, k, k_sib)
    stat = swap(own_stat, PLANE_GROUPS)
    v_picked = pick_theirs(where, v, "pick_values", PICK_VALUES_COST)
    v_sib = lax.ppermute(v_picked, BOTH, CORE_SWAP)

    def home(array, d):
        return lax.ppermute(array, BOTH, z_route(-d))

    part2, dq, lines = first_grads(2, where, msg, stat, k[2], v[2])
    pair2, dq = pair_grads(2, where, msg, lines, dq, k_sib, v_sib, (part2,))
    came2 = home(pair2, 2)
    pair1, dq = pair_grads(1, where, msg, lines, dq, k_sib, v_sib, (k[1], v[1]))
    came1 = home(pair1, 1)
    pair3, dq = pair_grads(3, where, msg, lines, dq, k_sib, v_sib, (k[3], v[3]))
    came3 = home(pair3, 3)
    own0, their02, dq = last_grads(where, msg, lines, dq, k_sib, v_sib, k[0], v[0], came2)
    dq = swap(dq.reshape(DEVICES, PAIRS, HEAD_DIM), None)
    from02 = lax.ppermute(their02, BOTH, CORE_SWAP)
    their1 = pick_theirs(where, [came1], "pick_1", JOIN_COST)
    from1 = lax.ppermute(their1, BOTH, CORE_SWAP)
    came3, _ = lax.optimization_barrier((came3, their1))
    their3 = pick_theirs(where, [came3], "pick_3", JOIN_COST)
    from3 = lax.ppermute(their3, BOTH, CORE_SWAP)
    outs = join_heads((0, 2), where, (own0, came2), ((from02, 0), (from02, 1)), ())
    outs = join_heads((1, 3), where, (came1, came3), ((from1, 0), (from3, 0)), outs)
    dq, outs = lax.optimization_barrier((dq, outs))
    return query_sum(dq), outs[0], outs[1]


def solution(mesh):
    return jax.shard_map(
        local,
        mesh=mesh,
        in_specs=(
            P(("pb", "ka"), None),
            P(("ka", "pb"), None),
            P(("ka", "pb"), None),
            P(("pb", "ka"), None),
            P(("pb", "ka"), None),
            P(),
        ),
        out_specs=(P(("pb", "ka"), None), P(("ka", "pb"), None), P(("ka", "pb"), None)),
        check_vma=False,
    )
```

```python
import functools
import math

import jax
import jax.numpy as jnp
from jax import lax
from jax.experimental import pallas as pl
from jax.experimental.pallas import tpu as pltpu
from jax.sharding import PartitionSpec as P

HEADS = 32
KV_HEADS = 8
HEAD_DIM = 128
PER_GROUP = HEADS // KV_HEADS
BOTH = ("pb", "ka")
DEVICES = 128
RINGS = 4
ROWS = 4
PAIRS = ROWS * PER_GROUP
MSG = 2 * PAIRS
PLANE = DEVICES // KV_HEADS
ALL_PAIRS = DEVICES * PAIRS
BLOCK = 512
EXTRA = 16
TALL = BLOCK + EXTRA
GRADS_COST = 0.1
GRAD_CHUNK = 1024
JOIN_COST = 0.3
STATS_COST = 0.1
FIRST_COST = 12
PICK_KEYS_COST = 10
PICK_VALUES_COST = 0.1
STAT = 24
MASKED = -1e30
SAFE = 2.0**60
LOG2E = math.log2(math.e)
INV_ROOT = 1.0 / math.sqrt(HEAD_DIM)
SCALE2 = INV_ROOT * LOG2E
CHUNK = 512
F32 = jnp.float32
BF16 = jnp.bfloat16
VMEM = pltpu.CompilerParams(vmem_limit_bytes=16 * 1024 * 1024)
LITTLE_VMEM = pltpu.CompilerParams(vmem_limit_bytes=6 * 1024 * 1024)
HBM = pl.BlockSpec(memory_space=pl.ANY)
RING_GROUPS = [[s * KV_HEADS + g for g in range(KV_HEADS)] for s in range(PLANE)]
PLANE_GROUPS = [[s * KV_HEADS + g for s in range(PLANE)] for g in range(KV_HEADS)]


def cost(microseconds):
    return pl.CostEstimate(
        flops=int(microseconds * 5e8), bytes_accessed=int(microseconds * 2e6), transcendentals=0
    )


SCALARS = pl.BlockSpec(memory_space=pltpu.SMEM)
WHOLE = pl.BlockSpec(memory_space=pltpu.VMEM)


def any_block(*shape):
    return pl.BlockSpec(shape, lambda i, w: (0,) * len(shape))


def block_first(pos_ref, d, other):
    place = lax.rem(pos_ref[0] + RINGS - d, RINGS) * 2 + (pos_ref[1] ^ other)
    return pos_ref[2] + place * (2 * BLOCK)


def place():
    ring = lax.rem(lax.axis_index("ka"), KV_HEADS)
    return ring // 2, lax.rem(ring, 2)


def column_copies(src, outs, sems):
    chip, _ = place()
    copies = []
    for step in range(KV_HEADS):
        d, core = step // 2, step % 2
        first = (lax.rem(chip + d, RINGS) * 2 + core) * HEAD_DIM
        cols = pl.ds(pl.multiple_of(first, HEAD_DIM), HEAD_DIM)
        copies.append(
            pltpu.make_async_copy(
                src.at[:, cols], outs[d].at[core, pl.ds(0, BLOCK)], sems.at[step]
            )
        )
    return copies


def split_values_kernel(v_ref, *rest):
    copies = column_copies(v_ref, rest[:-1], rest[-1])
    for copy in copies:
        copy.start()
    for copy in copies:
        copy.wait()


def split_values(values):
    return pl.pallas_call(
        split_values_kernel,
        out_specs=[HBM] * RINGS,
        scratch_shapes=[pltpu.SemaphoreType.DMA((KV_HEADS,))],
        out_shape=[jax.ShapeDtypeStruct((2, BLOCK, HEAD_DIM), BF16)] * RINGS,
        name="split_values",
        cost_estimate=cost(2),
    )(values)


def split_keys_kernel(k_ref, q_ref, do_ref, o_ref, *rest):
    outs, message_ref, (dots_ref, part_ref, sems, dots_sems, part_sems) = (
        rest[:RINGS],
        rest[RINGS],
        rest[RINGS + 1 :],
    )
    copies = column_copies(k_ref, outs, sems)
    for copy in copies:
        copy.start()
    chip, core = place()
    q = q_ref[...].astype(F32)
    do = do_ref[...].astype(F32)
    products = do * o_ref[...].astype(F32)
    row = lax.broadcasted_iota(jnp.int32, (ROWS, HEAD_DIM), 0)
    lane = lax.broadcasted_iota(jnp.int32, (ROWS, HEAD_DIM), 1) - (chip * 2 + core) * PAIRS
    for g in range(KV_HEADS):
        line = jnp.zeros((1, HEAD_DIM), F32)
        rows = [[], []]
        for j in range(PER_GROUP):
            first = (g * PER_GROUP + j) * HEAD_DIM
            cols = slice(first, first + HEAD_DIM)
            rows[0].append(q[:, cols])
            rows[1].append(do[:, cols])
            dots = jnp.sum(products[:, cols], axis=1, keepdims=True)
            placed = jnp.where(lane == row + j * ROWS, dots, 0.0)
            line += jnp.sum(placed, axis=0, keepdims=True)
        high = line.astype(BF16).astype(F32)
        rest_line = line - high
        middle = rest_line.astype(BF16).astype(F32)
        low = rest_line - middle
        lines = [high, middle, low, jnp.zeros((EXTRA - 3, HEAD_DIM), F32)]
        dots_ref[g // 2, g % 2] = jnp.concatenate(lines, axis=0).astype(BF16)
        part_ref[g] = jnp.concatenate(rows[0] + rows[1], axis=0).astype(BF16)
    last = [
        pltpu.make_async_copy(
            dots_ref.at[lax.rem(chip + d, RINGS)],
            outs[d].at[:, pl.ds(BLOCK, EXTRA)],
            dots_sems.at[d],
        )
        for d in range(RINGS)
    ]
    last += [
        pltpu.make_async_copy(part_ref, message_ref.at[s], part_sems.at[s]) for s in range(PLANE)
    ]
    for copy in last:
        copy.start()
    for copy in copies + last:
        copy.wait()


def split_keys(keys, queries, grad_out, out):
    return pl.pallas_call(
        split_keys_kernel,
        out_specs=[HBM] * (RINGS + 1),
        scratch_shapes=[
            pltpu.VMEM((RINGS, 2, EXTRA, HEAD_DIM), BF16),
            pltpu.VMEM((KV_HEADS, MSG, HEAD_DIM), BF16),
            pltpu.SemaphoreType.DMA((KV_HEADS,)),
            pltpu.SemaphoreType.DMA((RINGS,)),
            pltpu.SemaphoreType.DMA((PLANE,)),
        ],
        out_shape=[jax.ShapeDtypeStruct((2, TALL, HEAD_DIM), BF16)] * RINGS
        + [jax.ShapeDtypeStruct((PLANE, KV_HEADS, MSG, HEAD_DIM), BF16)],
        name="split_keys",
        cost_estimate=cost(2),
    )(keys, queries, grad_out, out)


def pick_kernel(where, *refs):
    for d, ref in enumerate(refs[:-1]):
        refs[-1][d] = ref[0]


def pick_theirs(where, arrived, name, time):
    rest = arrived[0].shape[1:]
    zeros = (0,) * len(rest)
    return pl.pallas_call(
        pick_kernel,
        grid_spec=pltpu.PrefetchScalarGridSpec(
            num_scalar_prefetch=1,
            grid=(1,),
            in_specs=[pl.BlockSpec((1,) + rest, lambda i, w: (1 - w[1],) + zeros)] * len(arrived),
            out_specs=any_block(len(arrived), *rest),
        ),
        out_shape=jax.ShapeDtypeStruct((len(arrived),) + rest, BF16),
        name=name,
        compiler_params=LITTLE_VMEM,
        cost_estimate=cost(time),
    )(where, *arrived)


def part_kernel(where, *refs):
    their_ref, mine_ref = refs[RINGS:]
    core = where[1]
    for d in range(RINGS):
        their_ref[d] = refs[d][1 - core]
        mine_ref[d] = refs[d][core]


def part_values(where, arrived):
    shape = jax.ShapeDtypeStruct((RINGS, BLOCK, HEAD_DIM), BF16)
    return pl.pallas_call(
        part_kernel,
        in_specs=[SCALARS] + [WHOLE] * RINGS,
        out_specs=[WHOLE, WHOLE],
        out_shape=[shape, shape],
        name="part_values",
        compiler_params=LITTLE_VMEM,
        cost_estimate=cost(PICK_VALUES_COST),
    )(where, *arrived)


def pair_positions(first, count, start):
    index = first + lax.broadcasted_iota(jnp.int32, (1, count), 1)
    return start + (index // PAIRS) * ROWS + lax.rem(index, ROWS)


def nt_dot(a, b):
    return lax.dot_general(a, b, (((1,), (1,)), ((), ())), preferred_element_type=F32)


def nn_dot(a, b):
    return lax.dot_general(a, b, (((1,), (0,)), ((), ())), preferred_element_type=F32)


def stats_kernel(pos_ref, msg_ref, *refs):
    mine_refs, sib_ref = refs[:RINGS], refs[RINGS]
    core = pos_ref[1]
    out_ref, mine_ref, top_ref, sum_ref, keys_ref, ready_ref = refs[RINGS + 1 :]
    start = pos_ref[3]
    top_ref[...] = jnp.full_like(top_ref, MASKED)
    sum_ref[...] = jnp.zeros_like(sum_ref)
    ready_ref[0] = 0
    terms = jnp.zeros((EXTRA, HEAD_DIM), F32)
    for d in range(RINGS):
        keys_ref[d] = mine_refs[d][core, 0:BLOCK]
        mine_ref[d] = mine_refs[d][core, 0:BLOCK]
        keys_ref[RINGS + d] = sib_ref[d, 0:BLOCK]
        terms += mine_refs[d][core, BLOCK:TALL].astype(F32) + sib_ref[d, BLOCK:TALL].astype(F32)

    def one(i, _):
        first = block_first(pos_ref, lax.rem(i, RINGS), i // RINGS)
        stats_step(
            first, start, msg_ref, lambda: keys_ref[i], top_ref, sum_ref, ready_ref
        )

    lax.fori_loop(0, KV_HEADS, one, None)
    bad = jnp.sum(jnp.where(sum_ref[...] < SAFE, 0.0, 1.0))

    @pl.when(bad > 0.0)
    def _():
        top_ref[...] = jnp.full_like(top_ref, MASKED)
        sum_ref[...] = jnp.zeros_like(sum_ref)
        ready_ref[0] = -1
        lax.fori_loop(0, KV_HEADS, one, None)

    total = sum_ref[...]
    logs = jnp.where(total > 0.0, top_ref[...] + jnp.log2(jnp.maximum(total, 1e-37)), MASKED)
    rows = [logs[:, r * HEAD_DIM : (r + 1) * HEAD_DIM] for r in range(PAIRS)]
    rows.append(terms[0:1] + terms[1:2] + terms[2:3])
    rows.append(jnp.zeros((STAT - PAIRS - 1, HEAD_DIM), F32))
    out = jnp.concatenate(rows, axis=0)
    for s in range(PLANE):
        out_ref[s] = out


def stats_step(first, start, msg_ref, load, top_ref, sum_ref, ready_ref):
    full = first + (BLOCK - 1) <= start
    some = first <= start + (DEVICES * ROWS - 1)

    def scores(c):
        devs = slice(c * CHUNK // PAIRS, (c + 1) * CHUNK // PAIRS)
        return nt_dot(load(), msg_ref[devs, 0:PAIRS].reshape(CHUNK, HEAD_DIM))

    def careful(masked):
        for c in range(ALL_PAIRS // CHUNK):
            cols = slice(c * CHUNK, (c + 1) * CHUNK)
            s = scores(c) * SCALE2
            if masked:
                key_pos = first + lax.broadcasted_iota(jnp.int32, (BLOCK, 1), 0)
                visible = key_pos <= pair_positions(c * CHUNK, CHUNK, start)
                s = jnp.where(visible, s, MASKED)
            old = top_ref[:, cols]
            top = jnp.maximum(old, jnp.max(s, axis=0, keepdims=True))
            e = jnp.exp2(s - top)
            if masked:
                e = jnp.where(visible, e, 0.0)
            sum_ref[:, cols] = sum_ref[:, cols] * jnp.exp2(old - top) + jnp.sum(
                e, axis=0, keepdims=True
            )
            top_ref[:, cols] = top

    quick = jnp.logical_and(full, ready_ref[0] == 1)

    @pl.when(quick)
    def _():
        for c in range(ALL_PAIRS // CHUNK):
            cols = slice(c * CHUNK, (c + 1) * CHUNK)
            e = jnp.exp2(scores(c) * SCALE2 - top_ref[:, cols])
            sum_ref[:, cols] += jnp.sum(e, axis=0, keepdims=True)

    @pl.when(jnp.logical_and(full, jnp.logical_not(quick)))
    def _():
        careful(False)
        ready_ref[0] = jnp.where(ready_ref[0] == 0, 1, ready_ref[0])

    @pl.when(jnp.logical_and(some, jnp.logical_not(full)))
    def _():
        careful(True)


def stats(pos, msg, mine, sib):
    row = pltpu.VMEM((1, ALL_PAIRS), F32)
    return pl.pallas_call(
        stats_kernel,
        in_specs=[SCALARS] + [WHOLE] * (2 + RINGS),
        out_specs=[WHOLE, WHOLE],
        scratch_shapes=[
            row,
            row,
            pltpu.VMEM((KV_HEADS, BLOCK, HEAD_DIM), BF16),
            pltpu.SMEM((1,), jnp.int32),
        ],
        out_shape=[
            jax.ShapeDtypeStruct((PLANE, STAT, HEAD_DIM), F32),
            jax.ShapeDtypeStruct((RINGS, BLOCK, HEAD_DIM), BF16),
        ],
        name="stats",
        compiler_params=VMEM,
        cost_estimate=cost(STATS_COST),
    )(pos, msg, *mine, sib)


def grad_blocks(pos_ref, msg_ref, lines_ref, blocks, sum_ref):
    start = pos_ref[3]
    firsts = [block_first(pos_ref, d, other) for _, _, d, other, _ in blocks]
    every = jnp.bool_(True)
    for first in firsts:
        every = jnp.logical_and(every, first + (BLOCK - 1) <= start)

    def run(which, masked, chunk):
        for first, (k_of, v_of, _, _, put) in which:
            k = k_of()
            v = v_of()
            k_turned = k.astype(F32).T.astype(BF16)

            def part(c, sums):
                dk, dv = sums
                at = c * chunk
                if masked:
                    at = pl.multiple_of(at, chunk)
                cols = pl.ds(at, chunk)
                devs = pl.ds(c * (chunk // PAIRS), chunk // PAIRS)
                q = msg_ref[devs, 0:PAIRS].reshape(chunk, HEAD_DIM)
                do = msg_ref[devs, PAIRS:MSG].reshape(chunk, HEAD_DIM)
                w = jnp.exp2(nt_dot(k, q) * SCALE2 - lines_ref[0:1, cols])
                if masked:
                    key_pos = first + lax.broadcasted_iota(jnp.int32, (BLOCK, 1), 0)
                    visible = key_pos <= pair_positions(at, chunk, start)
                    w = jnp.where(visible, w, 0.0)
                ds = (w * (nt_dot(v, do) - lines_ref[1:2, cols])).astype(BF16)
                sum_ref[:, cols] += nn_dot(k_turned, ds)
                return dk + nn_dot(ds, q), dv + nn_dot(w.astype(BF16), do)

            zero = jnp.zeros((BLOCK, HEAD_DIM), F32)
            sums = (zero, zero)
            if masked:
                sums = lax.fori_loop(0, ALL_PAIRS // chunk, part, sums)
            else:
                for c in range(ALL_PAIRS // chunk):
                    sums = part(c, sums)
            dk, dv = sums
            put((dk * INV_ROOT).astype(BF16), dv.astype(BF16))

    @pl.when(every)
    def _():
        run(list(zip(firsts, blocks)), False, GRAD_CHUNK)

    for one in zip(firsts, blocks):
        some = one[0] <= start + (DEVICES * ROWS - 1)

        @pl.when(jnp.logical_and(some, jnp.logical_not(every)))
        def _():
            run([one], True, CHUNK)

        @pl.when(jnp.logical_not(some))
        def _():
            zero = jnp.zeros((BLOCK, HEAD_DIM), BF16)
            one[1][-1](zero, zero)


PAIR_SHAPE = jax.ShapeDtypeStruct((2, 2, BLOCK, HEAD_DIM), BF16)
DQ_SHAPE = jax.ShapeDtypeStruct((HEAD_DIM, ALL_PAIRS), F32)


def first_kernel(d, pos_ref, msg_ref, stat_ref, k_ref, v_ref, g_ref, dq_ref, lines_ref):
    logs = stat_ref[:, 0:PAIRS]
    most = jnp.max(logs, axis=0)
    logs = most + jnp.log2(jnp.sum(jnp.exp2(logs - most), axis=0))
    for r in range(PLANE):
        cols = slice(r * HEAD_DIM, (r + 1) * HEAD_DIM)
        lines_ref[0:1, cols] = logs[r : r + 1]
        lines_ref[1:2, cols] = stat_ref[r, PAIRS : PAIRS + 1]
    dq_ref[...] = jnp.zeros_like(dq_ref)

    def put(dk, dv):
        g_ref[0, 0] = dk
        g_ref[0, 1] = dv

    mine = (lambda: k_ref[d], lambda: v_ref[d], d, 0, put)
    grad_blocks(pos_ref, msg_ref, lines_ref, [mine], dq_ref)


def first_grads(d, pos, msg, stat, k, v):
    return pl.pallas_call(
        functools.partial(first_kernel, d),
        in_specs=[SCALARS] + [WHOLE] * 4,
        out_specs=[WHOLE] * 3,
        out_shape=[
            jax.ShapeDtypeStruct((1, 2, BLOCK, HEAD_DIM), BF16),
            DQ_SHAPE,
            jax.ShapeDtypeStruct((8, ALL_PAIRS), F32),
        ],
        name="first_grads",
        compiler_params=VMEM,
        cost_estimate=cost(FIRST_COST),
    )(pos, msg, stat, k, v)


def pair_kernel(d, early, pos_ref, msg_ref, lines_ref, dq_in_ref, *refs):
    refs = list(refs)
    core = pos_ref[1]
    dq_ref, g_ref = refs[-1], refs[-2]
    dq_ref[...] = dq_in_ref[...]

    def put_at(slot):
        def put(dk, dv):
            g_ref[slot, 0] = dk
            g_ref[slot, 1] = dv

        return put

    ks_ref, vs_ref = refs[0], refs[1]
    blocks = [(lambda: ks_ref[d, 0:BLOCK], lambda: vs_ref[d], d, 1, put_at(1 - core))]
    if early:
        g_ref[core] = refs[2][0]
    else:
        k_ref, v_ref = refs[2], refs[3]
        blocks.append((lambda: k_ref[d], lambda: v_ref[d], d, 0, put_at(core)))
    grad_blocks(pos_ref, msg_ref, lines_ref, blocks, dq_ref)


def pair_grads(d, pos, msg, lines, dq, k_sib, v_sib, own):
    return pl.pallas_call(
        functools.partial(pair_kernel, d, len(own) == 1),
        in_specs=[SCALARS] + [WHOLE] * (5 + len(own)),
        out_specs=[WHOLE] * 2,
        out_shape=[PAIR_SHAPE, DQ_SHAPE],
        input_output_aliases={3: 1},
        name=f"pair_grads_{d}",
        compiler_params=VMEM,
        cost_estimate=cost(GRADS_COST),
    )(pos, msg, lines, dq, k_sib, v_sib, *own)


def last_kernel(pos_ref, msg_ref, lines_ref, dq_in_ref, ks_ref, vs_ref, k_ref, v_ref, came_ref, *refs):
    own_ref, their_ref, dq_ref, sum_ref = refs
    core = pos_ref[1]
    sum_ref[...] = dq_in_ref[...]
    their_ref[1] = came_ref[1 - core]

    def put_theirs(dk, dv):
        their_ref[0, 0] = dk
        their_ref[0, 1] = dv

    def put_own(dk, dv):
        own_ref[0, 0] = dk
        own_ref[0, 1] = dv

    theirs = (lambda: ks_ref[0, 0:BLOCK], lambda: vs_ref[0], 0, 1, put_theirs)
    mine = (lambda: k_ref[0], lambda: v_ref[0], 0, 0, put_own)
    grad_blocks(pos_ref, msg_ref, lines_ref, [theirs, mine], sum_ref)
    dq_ref[...] = sum_ref[...].T.astype(dq_ref.dtype)


def last_grads(pos, msg, lines, dq, k_sib, v_sib, k, v, came):
    return pl.pallas_call(
        last_kernel,
        in_specs=[SCALARS] + [WHOLE] * 8,
        out_specs=[WHOLE] * 3,
        scratch_shapes=[pltpu.VMEM((HEAD_DIM, ALL_PAIRS), F32)],
        out_shape=[
            jax.ShapeDtypeStruct((1, 2, BLOCK, HEAD_DIM), BF16),
            PAIR_SHAPE,
            jax.ShapeDtypeStruct((ALL_PAIRS, HEAD_DIM), BF16),
        ],
        name="last_grads",
        compiler_params=VMEM,
        cost_estimate=cost(GRADS_COST),
    )(pos, msg, lines, dq, k_sib, v_sib, k, v, came)


def join_kernel(chips, where, *refs):
    dk_ref, dv_ref, pair_ref, sems = refs[-4:]
    copies = []
    for n, d in enumerate(chips):
        for core, ref in ((where[1], refs[2 * n]), (1 - where[1], refs[2 * n + 1])):
            cols = pl.ds(pl.multiple_of(core * HEAD_DIM, HEAD_DIM), HEAD_DIM)
            pair_ref[n, 0, :, cols] = ref[0, 0].astype(F32)
            pair_ref[n, 1, :, cols] = ref[0, 1].astype(F32)
        first = lax.rem(where[0] + d, RINGS) * (2 * HEAD_DIM)
        cols = pl.ds(pl.multiple_of(first, 2 * HEAD_DIM), 2 * HEAD_DIM)
        for i, ref in enumerate((dk_ref, dv_ref)):
            copies.append(
                pltpu.make_async_copy(pair_ref.at[n, i], ref.at[:, cols], sems.at[n, i])
            )
            copies[-1].start()
    for copy in copies:
        copy.wait()


def join_heads(chips, where, parts, theirs, outs):
    shape = jax.ShapeDtypeStruct((BLOCK, KV_HEADS * HEAD_DIM), F32)
    operands, specs = [], []
    for part, (array, at) in zip(parts, theirs):
        operands += [part, array]
        if part.shape[0] == 2:
            specs.append(pl.BlockSpec((1, 2, BLOCK, HEAD_DIM), lambda i, w: (w[1], 0, 0, 0)))
        else:
            specs.append(any_block(1, 2, BLOCK, HEAD_DIM))
        specs.append(pl.BlockSpec((1, 2, BLOCK, HEAD_DIM), lambda i, w, at=at: (at, 0, 0, 0)))
    count = len(operands)
    return pl.pallas_call(
        functools.partial(join_kernel, chips),
        grid_spec=pltpu.PrefetchScalarGridSpec(
            num_scalar_prefetch=1,
            grid=(1,),
            in_specs=specs + [HBM] * len(outs),
            out_specs=[HBM, HBM],
            scratch_shapes=[
                pltpu.VMEM((2, 2, BLOCK, 2 * HEAD_DIM), F32),
                pltpu.SemaphoreType.DMA((2, 2)),
            ],
        ),
        out_shape=[shape, shape],
        input_output_aliases={1 + count: 0, 2 + count: 1} if outs else {},
        name=f"join_heads_{chips[0]}",
        compiler_params=VMEM,
        cost_estimate=cost(JOIN_COST),
    )(where, *operands, *outs)


def query_kernel(part_ref, out_ref):
    for g in range(KV_HEADS):
        total = part_ref[g].astype(F32)
        for s in range(1, DEVICES // KV_HEADS):
            total += part_ref[s * KV_HEADS + g].astype(F32)
        total = total * INV_ROOT
        for j in range(PER_GROUP):
            first = (g * PER_GROUP + j) * HEAD_DIM
            out_ref[:, first : first + HEAD_DIM] = total[j * ROWS : (j + 1) * ROWS]


def query_sum(parts):
    return pl.pallas_call(
        query_kernel,
        out_shape=jax.ShapeDtypeStruct((ROWS, HEADS * HEAD_DIM), F32),
        name="query_sum",
        compiler_params=VMEM,
    )(parts)


def swap(array, groups):
    return lax.all_to_all(array, BOTH, 0, 0, axis_index_groups=groups, tiled=True)


def z_route(turn):
    pairs = []
    for device in range(DEVICES):
        chip = (device // 2) % RINGS
        target = (chip + turn) % RINGS
        pairs.append((device, device + 2 * (target - chip)))
    return pairs


CORE_SWAP = [(device, device ^ 1) for device in range(DEVICES)]


def around(parts):
    return [parts[0]] + [lax.ppermute(parts[d], BOTH, z_route(d)) for d in range(1, RINGS)]


def local(queries, keys, values, grad_out, out, window_start):
    ka = lax.axis_index("ka")
    ring = lax.rem(ka, KV_HEADS)
    chip, core = ring // 2, lax.rem(ring, 2)
    first = ((ka - ring) * 2 + lax.axis_index("pb")) * BLOCK
    where = jnp.stack([chip, core, first, window_start[0]]).astype(jnp.int32)

    *k_parts, msg_out = split_keys(keys, queries, grad_out, out)
    k = around(k_parts)
    msg = swap(msg_out.reshape(DEVICES, MSG, HEAD_DIM), None)
    values, _ = lax.optimization_barrier((values, msg_out))
    v_parts = split_values(values)
    k, _ = lax.optimization_barrier((k, v_parts))
    v = around(v_parts)
    picked = pick_theirs(where, k, "pick_keys", PICK_KEYS_COST)
    k_sib = lax.ppermute(picked, BOTH, CORE_SWAP)
    msg, _ = lax.optimization_barrier((msg, picked))
    own_stat, k_mine = stats(where, msg, k, k_sib)
    stat = swap(own_stat, PLANE_GROUPS)
    v_picked, v_mine = part_values(where, v)
    v_sib = lax.ppermute(v_picked, BOTH, CORE_SWAP)

    def home(array, d):
        return lax.ppermute(array, BOTH, z_route(-d))

    part2, dq, lines = first_grads(2, where, msg, stat, k_mine, v_mine)
    pair2, dq = pair_grads(2, where, msg, lines, dq, k_sib, v_sib, (part2,))
    came2 = home(pair2, 2)
    pair1, dq = pair_grads(1, where, msg, lines, dq, k_sib, v_sib, (k_mine, v_mine))
    came1 = home(pair1, 1)
    pair3, dq = pair_grads(3, where, msg, lines, dq, k_sib, v_sib, (k_mine, v_mine))
    came3 = home(pair3, 3)
    own0, their02, dq = last_grads(where, msg, lines, dq, k_sib, v_sib, k_mine, v_mine, came2)
    dq = swap(dq.reshape(DEVICES, PAIRS, HEAD_DIM), None)
    from02 = lax.ppermute(their02, BOTH, CORE_SWAP)
    their1 = pick_theirs(where, [came1], "pick_1", JOIN_COST)
    from1 = lax.ppermute(their1, BOTH, CORE_SWAP)
    came3, _ = lax.optimization_barrier((came3, their1))
    their3 = pick_theirs(where, [came3], "pick_3", JOIN_COST)
    from3 = lax.ppermute(their3, BOTH, CORE_SWAP)
    outs = join_heads((0, 2), where, (own0, came2), ((from02, 0), (from02, 1)), ())
    outs = join_heads((1, 3), where, (came1, came3), ((from1, 0), (from3, 0)), outs)
    dq, outs = lax.optimization_barrier((dq, outs))
    return query_sum(dq), outs[0], outs[1]


def solution(mesh):
    return jax.shard_map(
        local,
        mesh=mesh,
        in_specs=(
            P(("pb", "ka"), None),
            P(("ka", "pb"), None),
            P(("ka", "pb"), None),
            P(("pb", "ka"), None),
            P(("pb", "ka"), None),
            P(),
        ),
        out_specs=(P(("pb", "ka"), None), P(("ka", "pb"), None), P(("ka", "pb"), None)),
        check_vma=False,
    )
```

```python
import functools
import math

import jax
import jax.numpy as jnp
from jax import lax
from jax.experimental import pallas as pl
from jax.experimental.pallas import tpu as pltpu
from jax.sharding import PartitionSpec as P

HEADS = 32
KV_HEADS = 8
HEAD_DIM = 128
PER_GROUP = HEADS // KV_HEADS
BOTH = ("pb", "ka")
DEVICES = 128
RINGS = 4
ROWS = 4
PAIRS = ROWS * PER_GROUP
MSG = 2 * PAIRS
PLANE = DEVICES // KV_HEADS
ALL_PAIRS = DEVICES * PAIRS
BLOCK = 512
EXTRA = 16
TALL = BLOCK + EXTRA
GRADS_COST = 0.1
GRAD_CHUNK = 1024
JOIN_COST = 0.3
STATS_COST = 0.1
FIRST_COST = 12
PICK_KEYS_COST = 10
PICK_VALUES_COST = 0.1
STAT = 24
MASKED = -1e30
SAFE = 2.0**60
LOG2E = math.log2(math.e)
INV_ROOT = 1.0 / math.sqrt(HEAD_DIM)
SCALE2 = INV_ROOT * LOG2E
CHUNK = 512
F32 = jnp.float32
BF16 = jnp.bfloat16
VMEM = pltpu.CompilerParams(vmem_limit_bytes=16 * 1024 * 1024)
LITTLE_VMEM = pltpu.CompilerParams(vmem_limit_bytes=6 * 1024 * 1024)
HBM = pl.BlockSpec(memory_space=pl.ANY)
RING_GROUPS = [[s * KV_HEADS + g for g in range(KV_HEADS)] for s in range(PLANE)]
PLANE_GROUPS = [[s * KV_HEADS + g for s in range(PLANE)] for g in range(KV_HEADS)]


def cost(microseconds):
    return pl.CostEstimate(
        flops=int(microseconds * 5e8), bytes_accessed=int(microseconds * 2e6), transcendentals=0
    )


SCALARS = pl.BlockSpec(memory_space=pltpu.SMEM)
WHOLE = pl.BlockSpec(memory_space=pltpu.VMEM)


def any_block(*shape):
    return pl.BlockSpec(shape, lambda i, w: (0,) * len(shape))


def block_first(pos_ref, d, other):
    place = lax.rem(pos_ref[0] + RINGS - d, RINGS) * 2 + (pos_ref[1] ^ other)
    return pos_ref[2] + place * (2 * BLOCK)


def place():
    ring = lax.rem(lax.axis_index("ka"), KV_HEADS)
    return ring // 2, lax.rem(ring, 2)


def column_copies(src, outs, sems):
    chip, _ = place()
    copies = []
    for step in range(KV_HEADS):
        d, core = step // 2, step % 2
        first = (lax.rem(chip + d, RINGS) * 2 + core) * HEAD_DIM
        cols = pl.ds(pl.multiple_of(first, HEAD_DIM), HEAD_DIM)
        copies.append(
            pltpu.make_async_copy(
                src.at[:, cols], outs[d].at[core, pl.ds(0, BLOCK)], sems.at[step]
            )
        )
    return copies


def split_values_kernel(v_ref, *rest):
    copies = column_copies(v_ref, rest[:-1], rest[-1])
    for copy in copies:
        copy.start()
    for copy in copies:
        copy.wait()


def split_values(values):
    return pl.pallas_call(
        split_values_kernel,
        out_specs=[HBM] * RINGS,
        scratch_shapes=[pltpu.SemaphoreType.DMA((KV_HEADS,))],
        out_shape=[jax.ShapeDtypeStruct((2, BLOCK, HEAD_DIM), BF16)] * RINGS,
        name="split_values",
        cost_estimate=cost(2),
    )(values)


def split_keys_kernel(k_ref, q_ref, do_ref, o_ref, *rest):
    outs, message_ref, (dots_ref, part_ref, sems, dots_sems, part_sems) = (
        rest[:RINGS],
        rest[RINGS],
        rest[RINGS + 1 :],
    )
    copies = column_copies(k_ref, outs, sems)
    for copy in copies:
        copy.start()
    chip, core = place()
    q = q_ref[...].astype(F32)
    do = do_ref[...].astype(F32)
    products = do * o_ref[...].astype(F32)
    row = lax.broadcasted_iota(jnp.int32, (ROWS, HEAD_DIM), 0)
    lane = lax.broadcasted_iota(jnp.int32, (ROWS, HEAD_DIM), 1) - (chip * 2 + core) * PAIRS
    for g in range(KV_HEADS):
        line = jnp.zeros((1, HEAD_DIM), F32)
        rows = [[], []]
        for j in range(PER_GROUP):
            first = (g * PER_GROUP + j) * HEAD_DIM
            cols = slice(first, first + HEAD_DIM)
            rows[0].append(q[:, cols])
            rows[1].append(do[:, cols])
            dots = jnp.sum(products[:, cols], axis=1, keepdims=True)
            placed = jnp.where(lane == row + j * ROWS, dots, 0.0)
            line += jnp.sum(placed, axis=0, keepdims=True)
        high = line.astype(BF16).astype(F32)
        rest_line = line - high
        middle = rest_line.astype(BF16).astype(F32)
        low = rest_line - middle
        lines = [high, middle, low, jnp.zeros((EXTRA - 3, HEAD_DIM), F32)]
        dots_ref[g // 2, g % 2] = jnp.concatenate(lines, axis=0).astype(BF16)
        part_ref[g] = jnp.concatenate(rows[0] + rows[1], axis=0).astype(BF16)
    last = [
        pltpu.make_async_copy(
            dots_ref.at[lax.rem(chip + d, RINGS)],
            outs[d].at[:, pl.ds(BLOCK, EXTRA)],
            dots_sems.at[d],
        )
        for d in range(RINGS)
    ]
    last += [
        pltpu.make_async_copy(part_ref, message_ref.at[s], part_sems.at[s]) for s in range(PLANE)
    ]
    for copy in last:
        copy.start()
    for copy in copies + last:
        copy.wait()


def split_keys(keys, queries, grad_out, out):
    return pl.pallas_call(
        split_keys_kernel,
        out_specs=[HBM] * (RINGS + 1),
        scratch_shapes=[
            pltpu.VMEM((RINGS, 2, EXTRA, HEAD_DIM), BF16),
            pltpu.VMEM((KV_HEADS, MSG, HEAD_DIM), BF16),
            pltpu.SemaphoreType.DMA((KV_HEADS,)),
            pltpu.SemaphoreType.DMA((RINGS,)),
            pltpu.SemaphoreType.DMA((PLANE,)),
        ],
        out_shape=[jax.ShapeDtypeStruct((2, TALL, HEAD_DIM), BF16)] * RINGS
        + [jax.ShapeDtypeStruct((PLANE, KV_HEADS, MSG, HEAD_DIM), BF16)],
        name="split_keys",
        cost_estimate=cost(2),
    )(keys, queries, grad_out, out)


def pick_kernel(where, *refs):
    for d, ref in enumerate(refs[:-1]):
        refs[-1][d] = ref[0]


def pick_theirs(where, arrived, name, time):
    rest = arrived[0].shape[1:]
    zeros = (0,) * len(rest)
    return pl.pallas_call(
        pick_kernel,
        grid_spec=pltpu.PrefetchScalarGridSpec(
            num_scalar_prefetch=1,
            grid=(1,),
            in_specs=[pl.BlockSpec((1,) + rest, lambda i, w: (1 - w[1],) + zeros)] * len(arrived),
            out_specs=any_block(len(arrived), *rest),
        ),
        out_shape=jax.ShapeDtypeStruct((len(arrived),) + rest, BF16),
        name=name,
        compiler_params=LITTLE_VMEM,
        cost_estimate=cost(time),
    )(where, *arrived)


def part_kernel(where, *refs):
    their_ref, mine_ref = refs[RINGS:]
    core = where[1]
    for d in range(RINGS):
        their_ref[d] = refs[d][1 - core]
        mine_ref[d] = refs[d][core]


def part_values(where, arrived):
    shape = jax.ShapeDtypeStruct((RINGS, BLOCK, HEAD_DIM), BF16)
    return pl.pallas_call(
        part_kernel,
        in_specs=[SCALARS] + [WHOLE] * RINGS,
        out_specs=[WHOLE, WHOLE],
        out_shape=[shape, shape],
        name="part_values",
        compiler_params=LITTLE_VMEM,
        cost_estimate=cost(PICK_VALUES_COST),
    )(where, *arrived)


def pair_positions(first, count, start):
    index = first + lax.broadcasted_iota(jnp.int32, (1, count), 1)
    return start + (index // PAIRS) * ROWS + lax.rem(index, ROWS)


def nt_dot(a, b):
    return lax.dot_general(a, b, (((1,), (1,)), ((), ())), preferred_element_type=F32)


def nn_dot(a, b):
    return lax.dot_general(a, b, (((1,), (0,)), ((), ())), preferred_element_type=F32)


def stats_kernel(pos_ref, msg_ref, *refs):
    mine_refs, sib_ref = refs[:RINGS], refs[RINGS]
    core = pos_ref[1]
    out_ref, mine_ref, top_ref, sum_ref, keys_ref, ready_ref = refs[RINGS + 1 :]
    start = pos_ref[3]
    top_ref[...] = jnp.full_like(top_ref, MASKED)
    sum_ref[...] = jnp.zeros_like(sum_ref)
    ready_ref[0] = 0
    terms = jnp.zeros((EXTRA, HEAD_DIM), F32)
    for d in range(RINGS):
        keys_ref[d] = mine_refs[d][core, 0:BLOCK]
        mine_ref[d] = mine_refs[d][core, 0:BLOCK]
        keys_ref[RINGS + d] = sib_ref[d, 0:BLOCK]
        terms += mine_refs[d][core, BLOCK:TALL].astype(F32) + sib_ref[d, BLOCK:TALL].astype(F32)

    def one(i, _):
        first = block_first(pos_ref, lax.rem(i, RINGS), i // RINGS)
        stats_step(
            first, start, msg_ref, lambda: keys_ref[i], top_ref, sum_ref, ready_ref
        )

    lax.fori_loop(0, KV_HEADS, one, None)
    bad = jnp.sum(jnp.where(sum_ref[...] < SAFE, 0.0, 1.0))

    @pl.when(bad > 0.0)
    def _():
        top_ref[...] = jnp.full_like(top_ref, MASKED)
        sum_ref[...] = jnp.zeros_like(sum_ref)
        ready_ref[0] = -1
        lax.fori_loop(0, KV_HEADS, one, None)

    total = sum_ref[...]
    logs = jnp.where(total > 0.0, top_ref[...] + jnp.log2(jnp.maximum(total, 1e-37)), MASKED)
    rows = [logs[:, r * HEAD_DIM : (r + 1) * HEAD_DIM] for r in range(PAIRS)]
    rows.append(terms[0:1] + terms[1:2] + terms[2:3])
    rows.append(jnp.zeros((STAT - PAIRS - 1, HEAD_DIM), F32))
    out = jnp.concatenate(rows, axis=0)
    for s in range(PLANE):
        out_ref[s] = out


def stats_step(first, start, msg_ref, load, top_ref, sum_ref, ready_ref):
    full = first + (BLOCK - 1) <= start
    some = first <= start + (DEVICES * ROWS - 1)

    def scores(c):
        devs = slice(c * CHUNK // PAIRS, (c + 1) * CHUNK // PAIRS)
        return nt_dot(load(), msg_ref[devs, 0:PAIRS].reshape(CHUNK, HEAD_DIM))

    def careful(masked):
        for c in range(ALL_PAIRS // CHUNK):
            cols = slice(c * CHUNK, (c + 1) * CHUNK)
            s = scores(c) * SCALE2
            if masked:
                key_pos = first + lax.broadcasted_iota(jnp.int32, (BLOCK, 1), 0)
                visible = key_pos <= pair_positions(c * CHUNK, CHUNK, start)
                s = jnp.where(visible, s, MASKED)
            old = top_ref[:, cols]
            top = jnp.maximum(old, jnp.max(s, axis=0, keepdims=True))
            e = jnp.exp2(s - top)
            if masked:
                e = jnp.where(visible, e, 0.0)
            sum_ref[:, cols] = sum_ref[:, cols] * jnp.exp2(old - top) + jnp.sum(
                e, axis=0, keepdims=True
            )
            top_ref[:, cols] = top

    quick = jnp.logical_and(full, ready_ref[0] == 1)

    @pl.when(quick)
    def _():
        for c in range(ALL_PAIRS // CHUNK):
            cols = slice(c * CHUNK, (c + 1) * CHUNK)
            e = jnp.exp2(scores(c) * SCALE2 - top_ref[:, cols])
            sum_ref[:, cols] += jnp.sum(e, axis=0, keepdims=True)

    @pl.when(jnp.logical_and(full, jnp.logical_not(quick)))
    def _():
        careful(False)
        ready_ref[0] = jnp.where(ready_ref[0] == 0, 1, ready_ref[0])

    @pl.when(jnp.logical_and(some, jnp.logical_not(full)))
    def _():
        careful(True)


def stats(pos, msg, mine, sib):
    row = pltpu.VMEM((1, ALL_PAIRS), F32)
    return pl.pallas_call(
        stats_kernel,
        in_specs=[SCALARS] + [WHOLE] * (2 + RINGS),
        out_specs=[WHOLE, WHOLE],
        scratch_shapes=[
            row,
            row,
            pltpu.VMEM((KV_HEADS, BLOCK, HEAD_DIM), BF16),
            pltpu.SMEM((1,), jnp.int32),
        ],
        out_shape=[
            jax.ShapeDtypeStruct((PLANE, STAT, HEAD_DIM), F32),
            jax.ShapeDtypeStruct((RINGS, BLOCK, HEAD_DIM), BF16),
        ],
        name="stats",
        compiler_params=VMEM,
        cost_estimate=cost(STATS_COST),
    )(pos, msg, *mine, sib)


def grad_blocks(pos_ref, msg_ref, lines_ref, blocks, sum_ref):
    start = pos_ref[3]
    firsts = [block_first(pos_ref, d, other) for _, _, d, other, _ in blocks]
    every = jnp.bool_(True)
    for first in firsts:
        every = jnp.logical_and(every, first + (BLOCK - 1) <= start)

    def run(which, masked, chunk):
        for first, (k_of, v_of, _, _, put) in which:
            k = k_of()
            v = v_of()
            k_turned = k.astype(F32).T.astype(BF16)

            def part(c, sums):
                dk, dv = sums
                at = c * chunk
                if masked:
                    at = pl.multiple_of(at, chunk)
                cols = pl.ds(at, chunk)
                devs = pl.ds(c * (chunk // PAIRS), chunk // PAIRS)
                q = msg_ref[devs, 0:PAIRS].reshape(chunk, HEAD_DIM)
                do = msg_ref[devs, PAIRS:MSG].reshape(chunk, HEAD_DIM)
                w = jnp.exp2(nt_dot(k, q) * SCALE2 - lines_ref[0:1, cols])
                if masked:
                    key_pos = first + lax.broadcasted_iota(jnp.int32, (BLOCK, 1), 0)
                    visible = key_pos <= pair_positions(at, chunk, start)
                    w = jnp.where(visible, w, 0.0)
                ds = (w * (nt_dot(v, do) - lines_ref[1:2, cols])).astype(BF16)
                sum_ref[:, cols] += nn_dot(k_turned, ds)
                return dk + nn_dot(ds, q), dv + nn_dot(w.astype(BF16), do)

            zero = jnp.zeros((BLOCK, HEAD_DIM), F32)
            sums = (zero, zero)
            if masked:
                sums = lax.fori_loop(0, ALL_PAIRS // chunk, part, sums)
            else:
                for c in range(ALL_PAIRS // chunk):
                    sums = part(c, sums)
            dk, dv = sums
            put((dk * INV_ROOT).astype(BF16), dv.astype(BF16))

    @pl.when(every)
    def _():
        run(list(zip(firsts, blocks)), False, GRAD_CHUNK)

    for one in zip(firsts, blocks):
        some = one[0] <= start + (DEVICES * ROWS - 1)

        @pl.when(jnp.logical_and(some, jnp.logical_not(every)))
        def _():
            run([one], True, CHUNK)

        @pl.when(jnp.logical_not(some))
        def _():
            zero = jnp.zeros((BLOCK, HEAD_DIM), BF16)
            one[1][-1](zero, zero)


PAIR_SHAPE = jax.ShapeDtypeStruct((2, 2, BLOCK, HEAD_DIM), BF16)
DQ_SHAPE = jax.ShapeDtypeStruct((HEAD_DIM, ALL_PAIRS), F32)


def first_kernel(d, pos_ref, msg_ref, stat_ref, k_ref, v_ref, g_ref, dq_ref, lines_ref):
    logs = stat_ref[:, 0:PAIRS]
    most = jnp.max(logs, axis=0)
    logs = most + jnp.log2(jnp.sum(jnp.exp2(logs - most), axis=0))
    for r in range(PLANE):
        cols = slice(r * HEAD_DIM, (r + 1) * HEAD_DIM)
        lines_ref[0:1, cols] = logs[r : r + 1]
        lines_ref[1:2, cols] = stat_ref[r, PAIRS : PAIRS + 1]
    dq_ref[...] = jnp.zeros_like(dq_ref)

    def put(dk, dv):
        g_ref[0, 0] = dk
        g_ref[0, 1] = dv

    mine = (lambda: k_ref[d], lambda: v_ref[d], d, 0, put)
    grad_blocks(pos_ref, msg_ref, lines_ref, [mine], dq_ref)


def first_grads(d, pos, msg, stat, k, v):
    return pl.pallas_call(
        functools.partial(first_kernel, d),
        in_specs=[SCALARS] + [WHOLE] * 4,
        out_specs=[WHOLE] * 3,
        out_shape=[
            jax.ShapeDtypeStruct((1, 2, BLOCK, HEAD_DIM), BF16),
            DQ_SHAPE,
            jax.ShapeDtypeStruct((8, ALL_PAIRS), F32),
        ],
        name="first_grads",
        compiler_params=VMEM,
        cost_estimate=cost(FIRST_COST),
    )(pos, msg, stat, k, v)


def pair_kernel(d, early, pos_ref, msg_ref, lines_ref, dq_in_ref, *refs):
    refs = list(refs)
    core = pos_ref[1]
    dq_ref, g_ref = refs[-1], refs[-2]
    dq_ref[...] = dq_in_ref[...]

    def put_at(slot):
        def put(dk, dv):
            g_ref[slot, 0] = dk
            g_ref[slot, 1] = dv

        return put

    ks_ref, vs_ref = refs[0], refs[1]
    blocks = [(lambda: ks_ref[d, 0:BLOCK], lambda: vs_ref[d], d, 1, put_at(1 - core))]
    if early:
        g_ref[core] = refs[2][0]
    else:
        k_ref, v_ref = refs[2], refs[3]
        blocks.append((lambda: k_ref[d], lambda: v_ref[d], d, 0, put_at(core)))
    grad_blocks(pos_ref, msg_ref, lines_ref, blocks, dq_ref)


def pair_grads(d, pos, msg, lines, dq, k_sib, v_sib, own):
    return pl.pallas_call(
        functools.partial(pair_kernel, d, len(own) == 1),
        in_specs=[SCALARS] + [WHOLE] * (5 + len(own)),
        out_specs=[WHOLE] * 2,
        out_shape=[PAIR_SHAPE, DQ_SHAPE],
        input_output_aliases={3: 1},
        name=f"pair_grads_{d}",
        compiler_params=VMEM,
        cost_estimate=cost(GRADS_COST),
    )(pos, msg, lines, dq, k_sib, v_sib, *own)


def last_kernel(pos_ref, msg_ref, lines_ref, dq_in_ref, ks_ref, vs_ref, k_ref, v_ref, came_ref, *refs):
    own_ref, their_ref, passed_ref, dq_ref, sum_ref = refs
    core = pos_ref[1]
    sum_ref[...] = dq_in_ref[...]
    passed_ref[0] = came_ref[1 - core]

    def put_theirs(dk, dv):
        their_ref[0, 0] = dk
        their_ref[0, 1] = dv

    def put_own(dk, dv):
        own_ref[0, 0] = dk
        own_ref[0, 1] = dv

    theirs = (lambda: ks_ref[0, 0:BLOCK], lambda: vs_ref[0], 0, 1, put_theirs)
    mine = (lambda: k_ref[0], lambda: v_ref[0], 0, 0, put_own)
    grad_blocks(pos_ref, msg_ref, lines_ref, [theirs, mine], sum_ref)
    dq_ref[...] = sum_ref[...].T.astype(dq_ref.dtype)


def last_grads(pos, msg, lines, dq, k_sib, v_sib, k, v, came):
    return pl.pallas_call(
        last_kernel,
        in_specs=[SCALARS] + [WHOLE] * 8,
        out_specs=[WHOLE] * 4,
        scratch_shapes=[pltpu.VMEM((HEAD_DIM, ALL_PAIRS), F32)],
        out_shape=[
            jax.ShapeDtypeStruct((1, 2, BLOCK, HEAD_DIM), BF16),
            jax.ShapeDtypeStruct((1, 2, BLOCK, HEAD_DIM), BF16),
            jax.ShapeDtypeStruct((1, 2, BLOCK, HEAD_DIM), BF16),
            jax.ShapeDtypeStruct((ALL_PAIRS, HEAD_DIM), BF16),
        ],
        name="last_grads",
        compiler_params=VMEM,
        cost_estimate=cost(GRADS_COST),
    )(pos, msg, lines, dq, k_sib, v_sib, k, v, came)


def join_kernel(chips, where, *refs):
    dk_ref, dv_ref, pair_ref, sems = refs[-4:]
    copies = []
    for n, d in enumerate(chips):
        for core, ref in ((where[1], refs[2 * n]), (1 - where[1], refs[2 * n + 1])):
            cols = pl.ds(pl.multiple_of(core * HEAD_DIM, HEAD_DIM), HEAD_DIM)
            pair_ref[n, 0, :, cols] = ref[0, 0].astype(F32)
            pair_ref[n, 1, :, cols] = ref[0, 1].astype(F32)
        first = lax.rem(where[0] + d, RINGS) * (2 * HEAD_DIM)
        cols = pl.ds(pl.multiple_of(first, 2 * HEAD_DIM), 2 * HEAD_DIM)
        for i, ref in enumerate((dk_ref, dv_ref)):
            copies.append(
                pltpu.make_async_copy(pair_ref.at[n, i], ref.at[:, cols], sems.at[n, i])
            )
            copies[-1].start()
    for copy in copies:
        copy.wait()


def join_heads(chips, where, parts, theirs, outs):
    shape = jax.ShapeDtypeStruct((BLOCK, KV_HEADS * HEAD_DIM), F32)
    operands, specs = [], []
    for part, (array, at) in zip(parts, theirs):
        operands += [part, array]
        if part.shape[0] == 2:
            specs.append(pl.BlockSpec((1, 2, BLOCK, HEAD_DIM), lambda i, w: (w[1], 0, 0, 0)))
        else:
            specs.append(any_block(1, 2, BLOCK, HEAD_DIM))
        specs.append(pl.BlockSpec((1, 2, BLOCK, HEAD_DIM), lambda i, w, at=at: (at, 0, 0, 0)))
    count = len(operands)
    return pl.pallas_call(
        functools.partial(join_kernel, chips),
        grid_spec=pltpu.PrefetchScalarGridSpec(
            num_scalar_prefetch=1,
            grid=(1,),
            in_specs=specs + [HBM] * len(outs),
            out_specs=[HBM, HBM],
            scratch_shapes=[
                pltpu.VMEM((2, 2, BLOCK, 2 * HEAD_DIM), F32),
                pltpu.SemaphoreType.DMA((2, 2)),
            ],
        ),
        out_shape=[shape, shape],
        input_output_aliases={1 + count: 0, 2 + count: 1} if outs else {},
        name=f"join_heads_{chips[0]}",
        compiler_params=VMEM,
        cost_estimate=cost(JOIN_COST),
    )(where, *operands, *outs)


def query_kernel(part_ref, out_ref):
    for g in range(KV_HEADS):
        total = part_ref[g].astype(F32)
        for s in range(1, DEVICES // KV_HEADS):
            total += part_ref[s * KV_HEADS + g].astype(F32)
        total = total * INV_ROOT
        for j in range(PER_GROUP):
            first = (g * PER_GROUP + j) * HEAD_DIM
            out_ref[:, first : first + HEAD_DIM] = total[j * ROWS : (j + 1) * ROWS]


def query_sum(parts):
    return pl.pallas_call(
        query_kernel,
        out_shape=jax.ShapeDtypeStruct((ROWS, HEADS * HEAD_DIM), F32),
        name="query_sum",
        compiler_params=VMEM,
    )(parts)


def swap(array, groups):
    return lax.all_to_all(array, BOTH, 0, 0, axis_index_groups=groups, tiled=True)


def z_route(turn):
    pairs = []
    for device in range(DEVICES):
        chip = (device // 2) % RINGS
        target = (chip + turn) % RINGS
        pairs.append((device, device + 2 * (target - chip)))
    return pairs


CORE_SWAP = [(device, device ^ 1) for device in range(DEVICES)]


def around(parts):
    return [parts[0]] + [lax.ppermute(parts[d], BOTH, z_route(d)) for d in range(1, RINGS)]


def local(queries, keys, values, grad_out, out, window_start):
    ka = lax.axis_index("ka")
    ring = lax.rem(ka, KV_HEADS)
    chip, core = ring // 2, lax.rem(ring, 2)
    first = ((ka - ring) * 2 + lax.axis_index("pb")) * BLOCK
    where = jnp.stack([chip, core, first, window_start[0]]).astype(jnp.int32)

    *k_parts, msg_out = split_keys(keys, queries, grad_out, out)
    k = around(k_parts)
    msg = swap(msg_out.reshape(DEVICES, MSG, HEAD_DIM), None)
    values, _ = lax.optimization_barrier((values, msg_out))
    v_parts = split_values(values)
    k, _ = lax.optimization_barrier((k, v_parts))
    v = around(v_parts)
    picked = pick_theirs(where, k, "pick_keys", PICK_KEYS_COST)
    k_sib = lax.ppermute(picked, BOTH, CORE_SWAP)
    msg, _ = lax.optimization_barrier((msg, picked))
    own_stat, k_mine = stats(where, msg, k, k_sib)
    stat = swap(own_stat, PLANE_GROUPS)
    v_picked, v_mine = part_values(where, v)
    v_sib = lax.ppermute(v_picked, BOTH, CORE_SWAP)

    def home(array, d):
        return lax.ppermute(array, BOTH, z_route(-d))

    part2, dq, lines = first_grads(2, where, msg, stat, k_mine, v_mine)
    pair2, dq = pair_grads(2, where, msg, lines, dq, k_sib, v_sib, (part2,))
    came2 = home(pair2, 2)
    pair1, dq = pair_grads(1, where, msg, lines, dq, k_sib, v_sib, (k_mine, v_mine))
    came1 = home(pair1, 1)
    pair3, dq = pair_grads(3, where, msg, lines, dq, k_sib, v_sib, (k_mine, v_mine))
    came3 = home(pair3, 3)
    own0, their0, their2, dq = last_grads(where, msg, lines, dq, k_sib, v_sib, k_mine, v_mine, came2)
    dq = swap(dq.reshape(DEVICES, PAIRS, HEAD_DIM), None)
    from0 = lax.ppermute(their0, BOTH, CORE_SWAP)
    from2 = lax.ppermute(their2, BOTH, CORE_SWAP)
    their1 = pick_theirs(where, [came1], "pick_1", JOIN_COST)
    from1 = lax.ppermute(their1, BOTH, CORE_SWAP)
    came3, _ = lax.optimization_barrier((came3, their1))
    their3 = pick_theirs(where, [came3], "pick_3", JOIN_COST)
    from3 = lax.ppermute(their3, BOTH, CORE_SWAP)
    outs = join_heads((0, 2), where, (own0, came2), ((from0, 0), (from2, 0)), ())
    outs = join_heads((1, 3), where, (came1, came3), ((from1, 0), (from3, 0)), outs)
    dq, outs = lax.optimization_barrier((dq, outs))
    return query_sum(dq), outs[0], outs[1]


def solution(mesh):
    return jax.shard_map(
        local,
        mesh=mesh,
        in_specs=(
            P(("pb", "ka"), None),
            P(("ka", "pb"), None),
            P(("ka", "pb"), None),
            P(("pb", "ka"), None),
            P(("pb", "ka"), None),
            P(),
        ),
        out_specs=(P(("pb", "ka"), None), P(("ka", "pb"), None), P(("ka", "pb"), None)),
        check_vma=False,
    )
```

```python
import functools
import math

import jax
import jax.numpy as jnp
from jax import lax
from jax.experimental import pallas as pl
from jax.experimental.pallas import tpu as pltpu
from jax.sharding import PartitionSpec as P

HEADS = 32
KV_HEADS = 8
HEAD_DIM = 128
PER_GROUP = HEADS // KV_HEADS
BOTH = ("pb", "ka")
DEVICES = 128
RINGS = 4
ROWS = 4
PAIRS = ROWS * PER_GROUP
MSG = 2 * PAIRS
PLANE = DEVICES // KV_HEADS
ALL_PAIRS = DEVICES * PAIRS
BLOCK = 512
EXTRA = 16
TALL = BLOCK + EXTRA
GRADS_COST = 0.1
GRAD_CHUNK = 1024
STATS_CHUNK = 1024
JOIN_COST = 0.3
STATS_COST = 0.1
FIRST_COST = 12
PICK_KEYS_COST = 10
PICK_VALUES_COST = 0.1
STAT = 24
MASKED = -1e30
SAFE = 2.0**60
LOG2E = math.log2(math.e)
INV_ROOT = 1.0 / math.sqrt(HEAD_DIM)
SCALE2 = INV_ROOT * LOG2E
CHUNK = 512
F32 = jnp.float32
BF16 = jnp.bfloat16
VMEM = pltpu.CompilerParams(vmem_limit_bytes=16 * 1024 * 1024)
LITTLE_VMEM = pltpu.CompilerParams(vmem_limit_bytes=6 * 1024 * 1024)
HBM = pl.BlockSpec(memory_space=pl.ANY)
RING_GROUPS = [[s * KV_HEADS + g for g in range(KV_HEADS)] for s in range(PLANE)]
PLANE_GROUPS = [[s * KV_HEADS + g for s in range(PLANE)] for g in range(KV_HEADS)]


def cost(microseconds):
    return pl.CostEstimate(
        flops=int(microseconds * 5e8), bytes_accessed=int(microseconds * 2e6), transcendentals=0
    )


SCALARS = pl.BlockSpec(memory_space=pltpu.SMEM)
WHOLE = pl.BlockSpec(memory_space=pltpu.VMEM)


def any_block(*shape):
    return pl.BlockSpec(shape, lambda i, w: (0,) * len(shape))


def block_first(pos_ref, d, other):
    place = lax.rem(pos_ref[0] + RINGS - d, RINGS) * 2 + (pos_ref[1] ^ other)
    return pos_ref[2] + place * (2 * BLOCK)


def place():
    ring = lax.rem(lax.axis_index("ka"), KV_HEADS)
    return ring // 2, lax.rem(ring, 2)


def column_copies(src, outs, sems):
    chip, _ = place()
    copies = []
    for step in range(KV_HEADS):
        d, core = step // 2, step % 2
        first = (lax.rem(chip + d, RINGS) * 2 + core) * HEAD_DIM
        cols = pl.ds(pl.multiple_of(first, HEAD_DIM), HEAD_DIM)
        copies.append(
            pltpu.make_async_copy(
                src.at[:, cols], outs[d].at[core, pl.ds(0, BLOCK)], sems.at[step]
            )
        )
    return copies


def split_values_kernel(v_ref, *rest):
    copies = column_copies(v_ref, rest[:-1], rest[-1])
    for copy in copies:
        copy.start()
    for copy in copies:
        copy.wait()


def split_values(values):
    return pl.pallas_call(
        split_values_kernel,
        out_specs=[HBM] * RINGS,
        scratch_shapes=[pltpu.SemaphoreType.DMA((KV_HEADS,))],
        out_shape=[jax.ShapeDtypeStruct((2, BLOCK, HEAD_DIM), BF16)] * RINGS,
        name="split_values",
        cost_estimate=cost(2),
    )(values)


def split_keys_kernel(k_ref, q_ref, do_ref, o_ref, *rest):
    outs, message_ref, (dots_ref, part_ref, sems, dots_sems, part_sems) = (
        rest[:RINGS],
        rest[RINGS],
        rest[RINGS + 1 :],
    )
    copies = column_copies(k_ref, outs, sems)
    for copy in copies:
        copy.start()
    chip, core = place()
    q = q_ref[...].astype(F32)
    do = do_ref[...].astype(F32)
    products = do * o_ref[...].astype(F32)
    row = lax.broadcasted_iota(jnp.int32, (ROWS, HEAD_DIM), 0)
    lane = lax.broadcasted_iota(jnp.int32, (ROWS, HEAD_DIM), 1) - (chip * 2 + core) * PAIRS
    for g in range(KV_HEADS):
        line = jnp.zeros((1, HEAD_DIM), F32)
        rows = [[], []]
        for j in range(PER_GROUP):
            first = (g * PER_GROUP + j) * HEAD_DIM
            cols = slice(first, first + HEAD_DIM)
            rows[0].append(q[:, cols])
            rows[1].append(do[:, cols])
            dots = jnp.sum(products[:, cols], axis=1, keepdims=True)
            placed = jnp.where(lane == row + j * ROWS, dots, 0.0)
            line += jnp.sum(placed, axis=0, keepdims=True)
        high = line.astype(BF16).astype(F32)
        rest_line = line - high
        middle = rest_line.astype(BF16).astype(F32)
        low = rest_line - middle
        lines = [high, middle, low, jnp.zeros((EXTRA - 3, HEAD_DIM), F32)]
        dots_ref[g // 2, g % 2] = jnp.concatenate(lines, axis=0).astype(BF16)
        part_ref[g] = jnp.concatenate(rows[0] + rows[1], axis=0).astype(BF16)
    last = [
        pltpu.make_async_copy(
            dots_ref.at[lax.rem(chip + d, RINGS)],
            outs[d].at[:, pl.ds(BLOCK, EXTRA)],
            dots_sems.at[d],
        )
        for d in range(RINGS)
    ]
    last += [
        pltpu.make_async_copy(part_ref, message_ref.at[s], part_sems.at[s]) for s in range(PLANE)
    ]
    for copy in last:
        copy.start()
    for copy in copies + last:
        copy.wait()


def split_keys(keys, queries, grad_out, out):
    return pl.pallas_call(
        split_keys_kernel,
        out_specs=[HBM] * (RINGS + 1),
        scratch_shapes=[
            pltpu.VMEM((RINGS, 2, EXTRA, HEAD_DIM), BF16),
            pltpu.VMEM((KV_HEADS, MSG, HEAD_DIM), BF16),
            pltpu.SemaphoreType.DMA((KV_HEADS,)),
            pltpu.SemaphoreType.DMA((RINGS,)),
            pltpu.SemaphoreType.DMA((PLANE,)),
        ],
        out_shape=[jax.ShapeDtypeStruct((2, TALL, HEAD_DIM), BF16)] * RINGS
        + [jax.ShapeDtypeStruct((PLANE, KV_HEADS, MSG, HEAD_DIM), BF16)],
        name="split_keys",
        cost_estimate=cost(2),
    )(keys, queries, grad_out, out)


def pick_kernel(where, *refs):
    for d, ref in enumerate(refs[:-1]):
        refs[-1][d] = ref[0]


def pick_theirs(where, arrived, name, time):
    rest = arrived[0].shape[1:]
    zeros = (0,) * len(rest)
    return pl.pallas_call(
        pick_kernel,
        grid_spec=pltpu.PrefetchScalarGridSpec(
            num_scalar_prefetch=1,
            grid=(1,),
            in_specs=[pl.BlockSpec((1,) + rest, lambda i, w: (1 - w[1],) + zeros)] * len(arrived),
            out_specs=any_block(len(arrived), *rest),
        ),
        out_shape=jax.ShapeDtypeStruct((len(arrived),) + rest, BF16),
        name=name,
        compiler_params=LITTLE_VMEM,
        cost_estimate=cost(time),
    )(where, *arrived)


def part_kernel(where, *refs):
    their_ref, mine_ref = refs[RINGS:]
    core = where[1]
    for d in range(RINGS):
        their_ref[d] = refs[d][1 - core]
        mine_ref[d] = refs[d][core]


def part_values(where, arrived):
    shape = jax.ShapeDtypeStruct((RINGS, BLOCK, HEAD_DIM), BF16)
    return pl.pallas_call(
        part_kernel,
        in_specs=[SCALARS] + [WHOLE] * RINGS,
        out_specs=[WHOLE, WHOLE],
        out_shape=[shape, shape],
        name="part_values",
        compiler_params=LITTLE_VMEM,
        cost_estimate=cost(PICK_VALUES_COST),
    )(where, *arrived)


def pair_positions(first, count, start):
    index = first + lax.broadcasted_iota(jnp.int32, (1, count), 1)
    return start + (index // PAIRS) * ROWS + lax.rem(index, ROWS)


def nt_dot(a, b):
    return lax.dot_general(a, b, (((1,), (1,)), ((), ())), preferred_element_type=F32)


def nn_dot(a, b):
    return lax.dot_general(a, b, (((1,), (0,)), ((), ())), preferred_element_type=F32)


def stats_kernel(pos_ref, msg_ref, *refs):
    mine_refs, sib_ref = refs[:RINGS], refs[RINGS]
    core = pos_ref[1]
    out_ref, mine_ref, top_ref, sum_ref, keys_ref, ready_ref = refs[RINGS + 1 :]
    start = pos_ref[3]
    top_ref[...] = jnp.full_like(top_ref, MASKED)
    sum_ref[...] = jnp.zeros_like(sum_ref)
    ready_ref[0] = 0
    terms = jnp.zeros((EXTRA, HEAD_DIM), F32)
    for d in range(RINGS):
        keys_ref[d] = mine_refs[d][core, 0:BLOCK]
        mine_ref[d] = mine_refs[d][core, 0:BLOCK]
        keys_ref[RINGS + d] = sib_ref[d, 0:BLOCK]
        terms += mine_refs[d][core, BLOCK:TALL].astype(F32) + sib_ref[d, BLOCK:TALL].astype(F32)

    def one(i, _):
        first = block_first(pos_ref, lax.rem(i, RINGS), i // RINGS)
        stats_step(
            first, start, msg_ref, lambda: keys_ref[i], top_ref, sum_ref, ready_ref
        )

    lax.fori_loop(0, KV_HEADS, one, None)
    bad = jnp.sum(jnp.where(sum_ref[...] < SAFE, 0.0, 1.0))

    @pl.when(bad > 0.0)
    def _():
        top_ref[...] = jnp.full_like(top_ref, MASKED)
        sum_ref[...] = jnp.zeros_like(sum_ref)
        ready_ref[0] = -1
        lax.fori_loop(0, KV_HEADS, one, None)

    total = sum_ref[...]
    logs = jnp.where(total > 0.0, top_ref[...] + jnp.log2(jnp.maximum(total, 1e-37)), MASKED)
    rows = [logs[:, r * HEAD_DIM : (r + 1) * HEAD_DIM] for r in range(PAIRS)]
    rows.append(terms[0:1] + terms[1:2] + terms[2:3])
    rows.append(jnp.zeros((STAT - PAIRS - 1, HEAD_DIM), F32))
    out = jnp.concatenate(rows, axis=0)
    for s in range(PLANE):
        out_ref[s] = out


def stats_step(first, start, msg_ref, load, top_ref, sum_ref, ready_ref):
    full = first + (BLOCK - 1) <= start
    some = first <= start + (DEVICES * ROWS - 1)

    def scores(c):
        devs = slice(c * STATS_CHUNK // PAIRS, (c + 1) * STATS_CHUNK // PAIRS)
        return nt_dot(load(), msg_ref[devs, 0:PAIRS].reshape(STATS_CHUNK, HEAD_DIM))

    def careful(masked):
        for c in range(ALL_PAIRS // STATS_CHUNK):
            cols = slice(c * STATS_CHUNK, (c + 1) * STATS_CHUNK)
            s = scores(c) * SCALE2
            if masked:
                key_pos = first + lax.broadcasted_iota(jnp.int32, (BLOCK, 1), 0)
                visible = key_pos <= pair_positions(c * STATS_CHUNK, STATS_CHUNK, start)
                s = jnp.where(visible, s, MASKED)
            old = top_ref[:, cols]
            top = jnp.maximum(old, jnp.max(s, axis=0, keepdims=True))
            e = jnp.exp2(s - top)
            if masked:
                e = jnp.where(visible, e, 0.0)
            sum_ref[:, cols] = sum_ref[:, cols] * jnp.exp2(old - top) + jnp.sum(
                e, axis=0, keepdims=True
            )
            top_ref[:, cols] = top

    quick = jnp.logical_and(full, ready_ref[0] == 1)

    @pl.when(quick)
    def _():
        for c in range(ALL_PAIRS // STATS_CHUNK):
            cols = slice(c * STATS_CHUNK, (c + 1) * STATS_CHUNK)
            e = jnp.exp2(scores(c) * SCALE2 - top_ref[:, cols])
            sum_ref[:, cols] += jnp.sum(e, axis=0, keepdims=True)

    @pl.when(jnp.logical_and(full, jnp.logical_not(quick)))
    def _():
        careful(False)
        ready_ref[0] = jnp.where(ready_ref[0] == 0, 1, ready_ref[0])

    @pl.when(jnp.logical_and(some, jnp.logical_not(full)))
    def _():
        careful(True)


def stats(pos, msg, mine, sib):
    row = pltpu.VMEM((1, ALL_PAIRS), F32)
    return pl.pallas_call(
        stats_kernel,
        in_specs=[SCALARS] + [WHOLE] * (2 + RINGS),
        out_specs=[WHOLE, WHOLE],
        scratch_shapes=[
            row,
            row,
            pltpu.VMEM((KV_HEADS, BLOCK, HEAD_DIM), BF16),
            pltpu.SMEM((1,), jnp.int32),
        ],
        out_shape=[
            jax.ShapeDtypeStruct((PLANE, STAT, HEAD_DIM), F32),
            jax.ShapeDtypeStruct((RINGS, BLOCK, HEAD_DIM), BF16),
        ],
        name="stats",
        compiler_params=VMEM,
        cost_estimate=cost(STATS_COST),
    )(pos, msg, *mine, sib)


def grad_blocks(pos_ref, msg_ref, lines_ref, blocks, sum_ref):
    start = pos_ref[3]
    firsts = [block_first(pos_ref, d, other) for _, _, d, other, _ in blocks]
    every = jnp.bool_(True)
    for first in firsts:
        every = jnp.logical_and(every, first + (BLOCK - 1) <= start)

    def run(which, masked, chunk):
        for first, (k_of, v_of, _, _, put) in which:
            k = k_of()
            v = v_of()
            k_turned = k.astype(F32).T.astype(BF16)

            def part(c, sums):
                dk, dv = sums
                at = c * chunk
                if masked:
                    at = pl.multiple_of(at, chunk)
                cols = pl.ds(at, chunk)
                devs = pl.ds(c * (chunk // PAIRS), chunk // PAIRS)
                q = msg_ref[devs, 0:PAIRS].reshape(chunk, HEAD_DIM)
                do = msg_ref[devs, PAIRS:MSG].reshape(chunk, HEAD_DIM)
                w = jnp.exp2(nt_dot(k, q) * SCALE2 - lines_ref[0:1, cols])
                if masked:
                    key_pos = first + lax.broadcasted_iota(jnp.int32, (BLOCK, 1), 0)
                    visible = key_pos <= pair_positions(at, chunk, start)
                    w = jnp.where(visible, w, 0.0)
                ds = (w * (nt_dot(v, do) - lines_ref[1:2, cols])).astype(BF16)
                sum_ref[:, cols] += nn_dot(k_turned, ds)
                return dk + nn_dot(ds, q), dv + nn_dot(w.astype(BF16), do)

            zero = jnp.zeros((BLOCK, HEAD_DIM), F32)
            sums = (zero, zero)
            if masked:
                sums = lax.fori_loop(0, ALL_PAIRS // chunk, part, sums)
            else:
                for c in range(ALL_PAIRS // chunk):
                    sums = part(c, sums)
            dk, dv = sums
            put((dk * INV_ROOT).astype(BF16), dv.astype(BF16))

    @pl.when(every)
    def _():
        run(list(zip(firsts, blocks)), False, GRAD_CHUNK)

    for one in zip(firsts, blocks):
        some = one[0] <= start + (DEVICES * ROWS - 1)

        @pl.when(jnp.logical_and(some, jnp.logical_not(every)))
        def _():
            run([one], True, CHUNK)

        @pl.when(jnp.logical_not(some))
        def _():
            zero = jnp.zeros((BLOCK, HEAD_DIM), BF16)
            one[1][-1](zero, zero)


PAIR_SHAPE = jax.ShapeDtypeStruct((2, 2, BLOCK, HEAD_DIM), BF16)
DQ_SHAPE = jax.ShapeDtypeStruct((HEAD_DIM, ALL_PAIRS), F32)


def first_kernel(d, pos_ref, msg_ref, stat_ref, k_ref, v_ref, g_ref, dq_ref, lines_ref):
    logs = stat_ref[:, 0:PAIRS]
    most = jnp.max(logs, axis=0)
    logs = most + jnp.log2(jnp.sum(jnp.exp2(logs - most), axis=0))
    for r in range(PLANE):
        cols = slice(r * HEAD_DIM, (r + 1) * HEAD_DIM)
        lines_ref[0:1, cols] = logs[r : r + 1]
        lines_ref[1:2, cols] = stat_ref[r, PAIRS : PAIRS + 1]
    dq_ref[...] = jnp.zeros_like(dq_ref)

    def put(dk, dv):
        g_ref[0, 0] = dk
        g_ref[0, 1] = dv

    mine = (lambda: k_ref[d], lambda: v_ref[d], d, 0, put)
    grad_blocks(pos_ref, msg_ref, lines_ref, [mine], dq_ref)


def first_grads(d, pos, msg, stat, k, v):
    return pl.pallas_call(
        functools.partial(first_kernel, d),
        in_specs=[SCALARS] + [WHOLE] * 4,
        out_specs=[WHOLE] * 3,
        out_shape=[
            jax.ShapeDtypeStruct((1, 2, BLOCK, HEAD_DIM), BF16),
            DQ_SHAPE,
            jax.ShapeDtypeStruct((8, ALL_PAIRS), F32),
        ],
        name="first_grads",
        compiler_params=VMEM,
        cost_estimate=cost(FIRST_COST),
    )(pos, msg, stat, k, v)


def pair_kernel(d, early, pos_ref, msg_ref, lines_ref, dq_in_ref, *refs):
    refs = list(refs)
    core = pos_ref[1]
    dq_ref, g_ref = refs[-1], refs[-2]
    dq_ref[...] = dq_in_ref[...]

    def put_at(slot):
        def put(dk, dv):
            g_ref[slot, 0] = dk
            g_ref[slot, 1] = dv

        return put

    ks_ref, vs_ref = refs[0], refs[1]
    blocks = [(lambda: ks_ref[d, 0:BLOCK], lambda: vs_ref[d], d, 1, put_at(1 - core))]
    if early:
        g_ref[core] = refs[2][0]
    else:
        k_ref, v_ref = refs[2], refs[3]
        blocks.append((lambda: k_ref[d], lambda: v_ref[d], d, 0, put_at(core)))
    grad_blocks(pos_ref, msg_ref, lines_ref, blocks, dq_ref)


def pair_grads(d, pos, msg, lines, dq, k_sib, v_sib, own):
    return pl.pallas_call(
        functools.partial(pair_kernel, d, len(own) == 1),
        in_specs=[SCALARS] + [WHOLE] * (5 + len(own)),
        out_specs=[WHOLE] * 2,
        out_shape=[PAIR_SHAPE, DQ_SHAPE],
        input_output_aliases={3: 1},
        name=f"pair_grads_{d}",
        compiler_params=VMEM,
        cost_estimate=cost(GRADS_COST),
    )(pos, msg, lines, dq, k_sib, v_sib, *own)


def last_kernel(pos_ref, msg_ref, lines_ref, dq_in_ref, ks_ref, vs_ref, k_ref, v_ref, came_ref, *refs):
    own_ref, their_ref, dq_ref, sum_ref = refs
    core = pos_ref[1]
    sum_ref[...] = dq_in_ref[...]
    their_ref[1] = came_ref[1 - core]

    def put_theirs(dk, dv):
        their_ref[0, 0] = dk
        their_ref[0, 1] = dv

    def put_own(dk, dv):
        own_ref[0, 0] = dk
        own_ref[0, 1] = dv

    theirs = (lambda: ks_ref[0, 0:BLOCK], lambda: vs_ref[0], 0, 1, put_theirs)
    mine = (lambda: k_ref[0], lambda: v_ref[0], 0, 0, put_own)
    grad_blocks(pos_ref, msg_ref, lines_ref, [theirs, mine], sum_ref)
    dq_ref[...] = sum_ref[...].T.astype(dq_ref.dtype)


def last_grads(pos, msg, lines, dq, k_sib, v_sib, k, v, came):
    return pl.pallas_call(
        last_kernel,
        in_specs=[SCALARS] + [WHOLE] * 8,
        out_specs=[WHOLE] * 3,
        scratch_shapes=[pltpu.VMEM((HEAD_DIM, ALL_PAIRS), F32)],
        out_shape=[
            jax.ShapeDtypeStruct((1, 2, BLOCK, HEAD_DIM), BF16),
            PAIR_SHAPE,
            jax.ShapeDtypeStruct((ALL_PAIRS, HEAD_DIM), BF16),
        ],
        name="last_grads",
        compiler_params=VMEM,
        cost_estimate=cost(GRADS_COST),
    )(pos, msg, lines, dq, k_sib, v_sib, k, v, came)


def join_kernel(chips, where, *refs):
    dk_ref, dv_ref, pair_ref, sems = refs[-4:]
    copies = []
    for n, d in enumerate(chips):
        for core, ref in ((where[1], refs[2 * n]), (1 - where[1], refs[2 * n + 1])):
            cols = pl.ds(pl.multiple_of(core * HEAD_DIM, HEAD_DIM), HEAD_DIM)
            pair_ref[n, 0, :, cols] = ref[0, 0].astype(F32)
            pair_ref[n, 1, :, cols] = ref[0, 1].astype(F32)
        first = lax.rem(where[0] + d, RINGS) * (2 * HEAD_DIM)
        cols = pl.ds(pl.multiple_of(first, 2 * HEAD_DIM), 2 * HEAD_DIM)
        for i, ref in enumerate((dk_ref, dv_ref)):
            copies.append(
                pltpu.make_async_copy(pair_ref.at[n, i], ref.at[:, cols], sems.at[n, i])
            )
            copies[-1].start()
    for copy in copies:
        copy.wait()


def join_heads(chips, where, parts, theirs, outs):
    shape = jax.ShapeDtypeStruct((BLOCK, KV_HEADS * HEAD_DIM), F32)
    operands, specs = [], []
    for part, (array, at) in zip(parts, theirs):
        operands += [part, array]
        if part.shape[0] == 2:
            specs.append(pl.BlockSpec((1, 2, BLOCK, HEAD_DIM), lambda i, w: (w[1], 0, 0, 0)))
        else:
            specs.append(any_block(1, 2, BLOCK, HEAD_DIM))
        specs.append(pl.BlockSpec((1, 2, BLOCK, HEAD_DIM), lambda i, w, at=at: (at, 0, 0, 0)))
    count = len(operands)
    return pl.pallas_call(
        functools.partial(join_kernel, chips),
        grid_spec=pltpu.PrefetchScalarGridSpec(
            num_scalar_prefetch=1,
            grid=(1,),
            in_specs=specs + [HBM] * len(outs),
            out_specs=[HBM, HBM],
            scratch_shapes=[
                pltpu.VMEM((2, 2, BLOCK, 2 * HEAD_DIM), F32),
                pltpu.SemaphoreType.DMA((2, 2)),
            ],
        ),
        out_shape=[shape, shape],
        input_output_aliases={1 + count: 0, 2 + count: 1} if outs else {},
        name=f"join_heads_{chips[0]}",
        compiler_params=VMEM,
        cost_estimate=cost(JOIN_COST),
    )(where, *operands, *outs)


def query_kernel(part_ref, out_ref):
    for g in range(KV_HEADS):
        total = part_ref[g].astype(F32)
        for s in range(1, DEVICES // KV_HEADS):
            total += part_ref[s * KV_HEADS + g].astype(F32)
        total = total * INV_ROOT
        for j in range(PER_GROUP):
            first = (g * PER_GROUP + j) * HEAD_DIM
            out_ref[:, first : first + HEAD_DIM] = total[j * ROWS : (j + 1) * ROWS]


def query_sum(parts):
    return pl.pallas_call(
        query_kernel,
        out_shape=jax.ShapeDtypeStruct((ROWS, HEADS * HEAD_DIM), F32),
        name="query_sum",
        compiler_params=VMEM,
    )(parts)


def swap(array, groups):
    return lax.all_to_all(array, BOTH, 0, 0, axis_index_groups=groups, tiled=True)


def z_route(turn):
    pairs = []
    for device in range(DEVICES):
        chip = (device // 2) % RINGS
        target = (chip + turn) % RINGS
        pairs.append((device, device + 2 * (target - chip)))
    return pairs


CORE_SWAP = [(device, device ^ 1) for device in range(DEVICES)]


def around(parts):
    return [parts[0]] + [lax.ppermute(parts[d], BOTH, z_route(d)) for d in range(1, RINGS)]


def local(queries, keys, values, grad_out, out, window_start):
    ka = lax.axis_index("ka")
    ring = lax.rem(ka, KV_HEADS)
    chip, core = ring // 2, lax.rem(ring, 2)
    first = ((ka - ring) * 2 + lax.axis_index("pb")) * BLOCK
    where = jnp.stack([chip, core, first, window_start[0]]).astype(jnp.int32)

    *k_parts, msg_out = split_keys(keys, queries, grad_out, out)
    k = around(k_parts)
    msg = swap(msg_out.reshape(DEVICES, MSG, HEAD_DIM), None)
    values, _ = lax.optimization_barrier((values, msg_out))
    v_parts = split_values(values)
    k, _ = lax.optimization_barrier((k, v_parts))
    v = around(v_parts)
    picked = pick_theirs(where, k, "pick_keys", PICK_KEYS_COST)
    k_sib = lax.ppermute(picked, BOTH, CORE_SWAP)
    msg, _ = lax.optimization_barrier((msg, picked))
    own_stat, k_mine = stats(where, msg, k, k_sib)
    stat = swap(own_stat, PLANE_GROUPS)
    v_picked, v_mine = part_values(where, v)
    v_sib = lax.ppermute(v_picked, BOTH, CORE_SWAP)

    def home(array, d):
        return lax.ppermute(array, BOTH, z_route(-d))

    part2, dq, lines = first_grads(2, where, msg, stat, k_mine, v_mine)
    pair2, dq = pair_grads(2, where, msg, lines, dq, k_sib, v_sib, (part2,))
    came2 = home(pair2, 2)
    pair1, dq = pair_grads(1, where, msg, lines, dq, k_sib, v_sib, (k_mine, v_mine))
    came1 = home(pair1, 1)
    pair3, dq = pair_grads(3, where, msg, lines, dq, k_sib, v_sib, (k_mine, v_mine))
    came3 = home(pair3, 3)
    own0, their02, dq = last_grads(where, msg, lines, dq, k_sib, v_sib, k_mine, v_mine, came2)
    dq = swap(dq.reshape(DEVICES, PAIRS, HEAD_DIM), None)
    from02 = lax.ppermute(their02, BOTH, CORE_SWAP)
    their1 = pick_theirs(where, [came1], "pick_1", JOIN_COST)
    from1 = lax.ppermute(their1, BOTH, CORE_SWAP)
    came3, _ = lax.optimization_barrier((came3, their1))
    their3 = pick_theirs(where, [came3], "pick_3", JOIN_COST)
    from3 = lax.ppermute(their3, BOTH, CORE_SWAP)
    outs = join_heads((0, 2), where, (own0, came2), ((from02, 0), (from02, 1)), ())
    outs = join_heads((1, 3), where, (came1, came3), ((from1, 0), (from3, 0)), outs)
    dq, outs = lax.optimization_barrier((dq, outs))
    return query_sum(dq), outs[0], outs[1]


def solution(mesh):
    return jax.shard_map(
        local,
        mesh=mesh,
        in_specs=(
            P(("pb", "ka"), None),
            P(("ka", "pb"), None),
            P(("ka", "pb"), None),
            P(("pb", "ka"), None),
            P(("pb", "ka"), None),
            P(),
        ),
        out_specs=(P(("pb", "ka"), None), P(("ka", "pb"), None), P(("ka", "pb"), None)),
        check_vma=False,
    )
```
